256 devices in a mesh: tile: 64 (over x, z, core), mode: 4 (over y).
Axes of the slice: x: 4, y: 4, z: 8, core: 2. Of those that a mesh axis runs over, the one named last changes fastest.
Arguments:
- object_tile: float32 [2, 384, 16384], P(None, None, 'tile'), may hold values from -6 to 6
- probe: float32 [12, 2, 256, 256], P('mode'), may hold values from -0.9 to 0.9
- amplitudes: float32 [128, 256, 256], P('tile'), may hold values from 0 to 2
- row_offsets: int32 [128], P('tile'), may hold values from 0 to 128
- col_offsets: int32 [128], P('tile'), may hold values from 0 to 255
- scan_count: int32 [64], P('tile'), may hold values from 1 to 2
Outputs:
- object_new: float32 [2, 384, 16384], P(None, None, 'tile')
- probe_new: float32 [12, 2, 256, 256], P('mode')
The draws below stay inside these ranges and needn't reach their ends.
All inputs are finite; a program needn't handle non-finite values.
Results may differ from the reference program's by a relative error of at most 0.011.
Values sent between devices are 32-bit elements; how exact they have to be, the bound alone decides.
A program may use at most 64 MiB of HBM per device.

```python
import jax
import jax.numpy as jnp
from jax import lax

P_SIZE = 256
MODES = 12
SCAN_DEV = 2
TH = 384
TW = 256
SCANS = 128
NX = 16384
N_TILE = 64


def plant(result, rng, low, high):
    index_at = [jax.random.randint(jax.random.fold_in(rng, axis), (), 0, length) for axis, length in enumerate(result.shape)]
    widest = result.shape.index(max(result.shape))
    neighbour = index_at[:widest] + [(index_at[widest] + 1) % result.shape[widest]] + index_at[widest + 1:]
    return result.at[tuple(index_at)].set(low).at[tuple(neighbour)].set(high)


def levels(stream_key, shape, cuts, least, largest):
    level = 1.0
    for dim, parts in cuts:
        steps = jax.random.uniform(jax.random.fold_in(jax.random.fold_in(stream_key, 6), dim), (parts,), jnp.float32, least / len(cuts), largest / len(cuts))
        level = level * jnp.repeat(jnp.exp(steps), shape[dim] // parts).reshape((-1,) + (1,) * (len(shape) - 1 - dim))
    return level


def normal_values(stream_key, dims, scale, most, split=(), kind=jnp.bfloat16):
    result = scale * jax.random.normal(stream_key, dims, jnp.float32)
    if split:
        result = result * levels(stream_key, dims, split, -0.22, 0.18)
    return jnp.clip(result, -most, most).astype(kind)


def setup_inputs(seed: int = 0) -> dict:
    key_of = jax.random.split(jax.random.key(seed), 7)
    object_tile = normal_values(key_of[0], (2, TH, NX), 1.0, 6.0, ((2, 64),), jnp.float32)
    probe = normal_values(key_of[1], (MODES, 2, P_SIZE, P_SIZE), 0.15, 0.9, ((0, 4),), jnp.float32)
    amplitudes = jnp.clip(2.0 * jax.random.uniform(key_of[2], (SCANS, P_SIZE, P_SIZE), jnp.float32) ** levels(key_of[2], (SCANS, P_SIZE, P_SIZE), ((0, 64),), -0.2, 0.2), 0.0, 2.0)
    row_offsets = plant(jax.random.randint(key_of[3], (SCANS,), 0, TH - P_SIZE + 1), jax.random.fold_in(key_of[3], 1), 0, TH - P_SIZE).astype(jnp.int32)
    col_offsets = plant(jax.random.randint(key_of[4], (SCANS,), 0, TW), jax.random.fold_in(key_of[4], 1), 0, TW - 1).astype(jnp.int32)
    scan_count = plant(jax.random.randint(key_of[5], (N_TILE,), 1, SCAN_DEV + 1), jax.random.fold_in(key_of[5], 1), 1, SCAN_DEV).astype(jnp.int32)
    return dict(object_tile=object_tile, probe=probe, amplitudes=amplitudes, row_offsets=row_offsets, col_offsets=col_offsets, scan_count=scan_count)


def dft_tables(length, sign):
    counter = jnp.arange(length, dtype=jnp.int32)
    phase = (jnp.outer(counter, counter) % length).astype(jnp.float32) * (2.0 * jnp.pi / length)
    scale = 1.0 / jnp.sqrt(jnp.float32(length))
    return ((jnp.cos(phase) * scale).astype(jnp.bfloat16), (sign * jnp.sin(phase) * scale).astype(jnp.bfloat16))

def to_half(value):
    return lax.optimization_barrier(value.astype(jnp.bfloat16)).astype(jnp.float32)

def apply_left(table, wave):
    return jnp.einsum('kn,mnj->mkj', table, wave, precision=lax.Precision.HIGHEST)

def apply_right(wave, table):
    return jnp.einsum('mkn,nj->mkj', wave, table, precision=lax.Precision.HIGHEST)

def transform(wave_real, wave_imag, table_real, table_imag):
    table_real = table_real.astype(jnp.float32)
    table_imag = table_imag.astype(jnp.float32)
    mid_real = to_half(apply_left(table_real, wave_real) - apply_left(table_imag, wave_imag))
    mid_imag = to_half(apply_left(table_real, wave_imag) + apply_left(table_imag, wave_real))
    out_real = apply_right(mid_real, table_real) - apply_right(mid_imag, table_imag)
    out_imag = apply_right(mid_real, table_imag) + apply_right(mid_imag, table_real)
    return (out_real, out_imag)

def reference(object_tile, probe, amplitudes, row_offsets, col_offsets, scan_count):
    fwd_real, fwd_imag = dft_tables(P_SIZE, -1.0)
    inv_real, inv_imag = dft_tables(P_SIZE, 1.0)
    padded = jnp.pad(object_tile, ((0, 0), (0, 0), (0, P_SIZE)))
    probe_real = probe[:, 0]
    probe_imag = probe[:, 1]

    def one_scan(carry, index):
        grid_sum, probe_sum = carry
        owner = (index // SCAN_DEV).astype(jnp.int32)
        start = (owner * TW + col_offsets[index]).astype(jnp.int32)
        top = row_offsets[index].astype(jnp.int32)
        zero = jnp.int32(0)
        window = lax.dynamic_slice(padded, (zero, top, start), (2, P_SIZE, P_SIZE))
        obj_real = window[0]
        obj_imag = window[1]
        psi_real = to_half(probe_real * obj_real - probe_imag * obj_imag)
        psi_imag = to_half(probe_real * obj_imag + probe_imag * obj_real)
        spec_real, spec_imag = transform(psi_real, psi_imag, fwd_real, fwd_imag)
        spec_real = to_half(spec_real)
        spec_imag = to_half(spec_imag)
        intensity = lax.optimization_barrier(jnp.sum(spec_real * spec_real + spec_imag * spec_imag, axis=0))
        factor = amplitudes[index] / jnp.maximum(jnp.sqrt(intensity), 0.5) - 1.0
        change_real = to_half(spec_real * factor)
        change_imag = to_half(spec_imag * factor)
        chi_real, chi_imag = transform(change_real, change_imag, inv_real, inv_imag)
        active = (index % SCAN_DEV < scan_count[owner]).astype(jnp.float32)
        grad_real = lax.optimization_barrier(jnp.sum(probe_real * chi_real + probe_imag * chi_imag, axis=0))
        grad_imag = lax.optimization_barrier(jnp.sum(probe_real * chi_imag - probe_imag * chi_real, axis=0))
        update = active * jnp.stack([grad_real, grad_imag])
        current = lax.dynamic_slice(grid_sum, (zero, top, start), (2, P_SIZE, P_SIZE))
        grid_sum = lax.dynamic_update_slice(grid_sum, current + update, (zero, top, start))
        pgrad_real = obj_real * chi_real + obj_imag * chi_imag
        pgrad_imag = obj_real * chi_imag - obj_imag * chi_real
        probe_sum = probe_sum + active * jnp.stack([pgrad_real, pgrad_imag], axis=1)
        return ((grid_sum, probe_sum), None)
    start_grid = jnp.zeros(padded.shape, jnp.float32)
    start_probe = jnp.zeros(probe.shape, jnp.float32)
    (grid_sum, probe_sum), unused = lax.scan(one_scan, (start_grid, start_probe), jnp.arange(SCANS, dtype=jnp.int32))
    object_new = object_tile + grid_sum[:, :, :NX]
    probe_new = probe + probe_sum / SCAN_DEV
    return (object_new, probe_new)
```

```python
import functools

import jax
import jax.numpy as jnp
import numpy as np
from jax import lax
from jax.experimental import pallas as pl
from jax.experimental.pallas import tpu as pltpu
from jax.sharding import PartitionSpec as P

SIDE = 256
ROWS = 384
MODES = 3
SCANS = 2
NX, NZ, NY = 4, 8, 4
N_TILE = 64
F32 = jnp.float32
BF16 = jnp.bfloat16
BLK = 32


def dft_blocks():
    counter = np.arange(SIDE)
    phase = (np.outer(counter, counter) % SIDE) * (2.0 * np.pi / SIDE)
    real = np.cos(phase) / np.sqrt(SIDE)
    imag = -np.sin(phase) / np.sqrt(SIDE)
    left = np.block([[real, -imag], [imag, real]])
    right = np.block([[real, imag], [-imag, real]])
    return left.astype(np.float32).astype(jnp.bfloat16), right.astype(np.float32).astype(jnp.bfloat16)


class Sems:
    def __init__(self, send, recv):
        self.send, self.recv, self.used, self.started = send, recv, 0, []

    def start(self, src, dst, dev):
        i = self.used
        self.used += 1
        copy = pltpu.make_async_remote_copy(
            src_ref=src,
            dst_ref=dst,
            send_sem=self.send.at[i],
            recv_sem=self.recv.at[i],
            device_id=dev,
            device_id_type=pl.DeviceIdType.MESH,
        )
        copy.start()
        self.started.append(copy)
        return copy


N_SEMS = 64


def rows(start, size):
    return pl.ds(pl.multiple_of(start, 8), size)


def aligned(first):
    base = jnp.minimum(first // 8, 15)
    return base, (BLK + 8 - (first - base * 8)) % (BLK + 8)


def kernel(
    where_ref, active_ref, obj_ref, probe_ref, amp_ref, lf_ref, rf_ref,
    onew_ref, pnew_ref,
    border, win, psi, half, spec, power, pw_a, pw_b, factor, pad, pgrad, p_core,
    px1, px2, pz, own, edge, ro1, ro2, re1, re2, arrive,
    send_sem, recv_sem,
):
    t = lax.axis_index("tile")
    y = lax.axis_index("mode")
    core = t % 2
    z = (t // 2) % NZ
    x = t // (2 * NZ)
    sems = Sems(send_sem, recv_sem)

    def tile_dev(xx, zz, cc):
        return ((xx * NZ + zz) * 2 + cc, y)

    t_left = ((t + N_TILE - 1) % N_TILE, y)
    t_right = ((t + 1) % N_TILE, y)
    peer = tile_dev(x, z, 1 - core)

    def pairs(i):
        return (i + 1 - 2 * (i % 2), 3 - i, ((i + 1) // 2) % 2, i // 2)

    ya, yb, yha, yhb = pairs(y)
    xa, xb, xha, xhb = pairs(x)
    y_dev = ((t, ya), (t, yb))
    x_dev = (tile_dev(xa, z, core), tile_dev(xb, z, core))
    y_half = (yha, yhb)
    x_half = (xha, xhb)
    z_dev = [tile_dev(x, (z + k) % NZ, core) for k in range(1, NZ)]

    barrier = pltpu.get_barrier_semaphore()
    partners = [t_left, t_right, *y_dev, *x_dev, *z_dev]
    for dev in partners:
        pl.semaphore_signal(barrier, inc=1, device_id=dev, device_id_type=pl.DeviceIdType.MESH)
    pl.semaphore_wait(barrier, len(partners))

    get_border = sems.start(obj_ref, border, t_left)
    for s in range(SCANS):
        for c in range(2):
            pad[s, c, 0:16] = jnp.zeros((16, 8, SIDE), F32)
            pad[s, c, 48:64] = jnp.zeros((16, 8, SIDE), F32)
    get_border.wait_recv()

    @pl.when(t == N_TILE - 1)
    def _():
        border[...] = jnp.zeros(border.shape, F32)

    def forward(s):
        base, up, shift = where_ref[0, s], where_ref[1, s], where_ref[4, s]

        def cut(i, carry):
            for c in range(2):
                at = pl.ds(base + i * (BLK // 8), BLK // 8 + 1)
                wide = jnp.concatenate([obj_ref[c, at], border[c, at]], axis=2).reshape(BLK + 8, 2 * SIDE)
                wide = pltpu.roll(wide, up, axis=0)[:BLK]
                win[s, c, rows(i * BLK, BLK), :] = pltpu.roll(wide, shift, axis=1)[:, :SIDE]
            return carry

        lax.fori_loop(0, SIDE // BLK, cut, 0)

        def mode(m, carry):
            pr = probe_ref[rows(m * 2 * SIDE, SIDE), :]
            pi = probe_ref[rows(m * 2 * SIDE + SIDE, SIDE), :]
            wr, wi = win[s, 0], win[s, 1]
            psi[0:SIDE, :] = (pr * wr - pi * wi).astype(BF16)
            psi[SIDE:, :] = (pr * wi + pi * wr).astype(BF16)
            mid = jnp.dot(lf_ref[...], psi[...], preferred_element_type=F32).astype(BF16)
            half[:, 0:SIDE] = mid[0:SIDE]
            half[:, SIDE:] = mid[SIDE:]
            out = jnp.dot(half[...], rf_ref[...], preferred_element_type=F32).astype(BF16)
            spec[s, m] = out
            wide = out.astype(F32)
            wide = wide * wide
            power[s] = jnp.where(m == 0, 0.0, power[s]) + wide[:, :SIDE] + wide[:, SIDE:]
            return carry

        lax.fori_loop(0, MODES, mode, 0)

    def order(s):
        return (s, 1 - s)

    step1, step2 = [], []
    for s in range(SCANS):
        forward(s)
        first, _ = order(s)
        h = y_half[first]
        step1.append(sems.start(power.at[s, rows((1 - h) * 128, 128), :], pw_a.at[s], y_dev[first]))
    quarter = []
    for s in range(SCANS):
        first, second = order(s)
        h, g = y_half[first], y_half[second]
        base = h * 128
        step1[s].wait_recv()
        power[s, rows(base, 128), :] = power[s, rows(base, 128), :] + pw_a[s]
        step2.append(sems.start(power.at[s, rows(base + (1 - g) * 64, 64), :], pw_b.at[s], y_dev[second]))
        quarter.append(base + g * 64)
    gather1, gather2 = [], []
    for s in range(SCANS):
        first, second = order(s)
        q = rows(quarter[s], 64)
        step2[s].wait_recv()
        total = power[s, q, :] + pw_b[s]
        factor[s, q, :] = amp_ref[s, q, :] / jnp.maximum(jnp.sqrt(total), 0.5) - 1.0
        gather1.append(sems.start(factor.at[s, q, :], factor.at[s, q, :], y_dev[second]))
    for s in range(SCANS):
        first, second = order(s)
        q = rows(y_half[first] * 128, 128)
        gather1[s].wait_recv()
        gather2.append(sems.start(factor.at[s, q, :], factor.at[s, q, :], y_dev[first]))

    def backward(s):
        active = active_ref[s]

        def mode(m, carry):
            f = factor[s]
            psi[0:SIDE, :] = (spec[s, m, :, :SIDE].astype(F32) * f).astype(BF16)
            psi[SIDE:, :] = (spec[s, m, :, SIDE:].astype(F32) * f).astype(BF16)
            mid = jnp.dot(rf_ref[...], psi[...], preferred_element_type=F32).astype(BF16)
            half[:, 0:SIDE] = mid[0:SIDE]
            half[:, SIDE:] = mid[SIDE:]
            chi = jnp.dot(half[...], lf_ref[...], preferred_element_type=F32) * active
            cr, ci = chi[:, :SIDE], chi[:, SIDE:]
            at_r, at_i = rows(m * 2 * SIDE, SIDE), rows(m * 2 * SIDE + SIDE, SIDE)
            pr, pi = probe_ref[at_r, :], probe_ref[at_i, :]
            wr, wi = win[s, 0], win[s, 1]
            gr = (pr * cr + pi * ci).reshape(SIDE // 8, 8, SIDE)
            gi = (pr * ci - pi * cr).reshape(SIDE // 8, 8, SIDE)
            pad[s, 0, 16:48] = jnp.where(m == 0, 0.0, pad[s, 0, 16:48]) + gr
            pad[s, 1, 16:48] = jnp.where(m == 0, 0.0, pad[s, 1, 16:48]) + gi
            if s == 0:
                pgrad[at_r, :] = wr * cr + wi * ci
                pgrad[at_i, :] = wr * ci - wi * cr
            else:
                pgrad[at_r, :] = pgrad[at_r, :] + wr * cr + wi * ci
                pgrad[at_i, :] = pgrad[at_i, :] + wr * ci - wi * cr
            return carry

        lax.fori_loop(0, MODES, mode, 0)

    for s in range(SCANS):
        gather2[s].wait_recv()
        backward(s)

    n_core = MODES * SIDE
    mine = core * n_core
    core_copy = sems.start(pgrad.at[rows((1 - core) * n_core, n_core), :], p_core, peer)

    def place(i, carry):
        for c in range(2):
            total = None
            for s in range(SCANS):
                base, up = where_ref[2, s], where_ref[3, s]
                block = pad[s, c, pl.ds(base + i * (BLK // 8), BLK // 8 + 1)].reshape(BLK + 8, SIDE)
                block = pltpu.roll(block, up, axis=0)[:BLK]
                wide = jnp.concatenate([block, jnp.zeros((BLK, SIDE), F32)], axis=1)
                wide = pltpu.roll(wide, where_ref[5, s], axis=1)
                total = wide if total is None else total + wide
            own[c, rows(i * BLK, BLK), :] = total[:, :SIDE]
            edge[c, rows(i * BLK, BLK), :] = total[:, SIDE:]
        return carry

    lax.fori_loop(0, ROWS // BLK, place, 0)

    half_rows, quarter_rows = ROWS // 2, ROWS // 4

    def reduce_1(grid, landing):
        copies = []
        for c in range(2):
            h = y_half[order(c)[0]]
            copies.append(
                sems.start(grid.at[c, rows((1 - h) * half_rows, half_rows), :], landing.at[c], y_dev[order(c)[0]])
            )
        return copies

    def reduce_2(grid, landing_1, landing_2, copies):
        result = []
        for c in range(2):
            first, second = order(c)
            h, g = y_half[first], y_half[second]
            base = h * half_rows
            copies[c].wait_recv()
            grid[c, rows(base, half_rows), :] = grid[c, rows(base, half_rows), :] + landing_1[c]
            result.append(
                sems.start(
                    grid.at[c, rows(base + (1 - g) * quarter_rows, quarter_rows), :], landing_2.at[c], y_dev[second]
                )
            )
        return result

    def quarter_at(c):
        first, second = order(c)
        return y_half[first] * half_rows + y_half[second] * quarter_rows

    def quarter_of(c):
        return rows(quarter_at(c), quarter_rows)

    edge_1 = reduce_1(edge, re1)
    own_1 = reduce_1(own, ro1)

    core_copy.wait_recv()
    pgrad[rows(mine, n_core), :] = pgrad[rows(mine, n_core), :] + p_core[...]
    n_part, n_half, n_quarter = n_core // 2, n_core // 4, n_core // 8
    x_1 = []
    for k in range(2):
        first, _ = order(k)
        x_1.append(
            sems.start(
                pgrad.at[rows(mine + k * n_part + (1 - x_half[first]) * n_half, n_half), :], px1.at[k], x_dev[first]
            )
        )

    edge_2 = reduce_2(edge, re1, re2, edge_1)

    x_2, x_at = [], []
    for k in range(2):
        first, second = order(k)
        base = mine + k * n_part + x_half[first] * n_half
        x_1[k].wait_recv()
        pgrad[rows(base, n_half), :] = pgrad[rows(base, n_half), :] + px1[k]
        x_2.append(
            sems.start(pgrad.at[rows(base + (1 - x_half[second]) * n_quarter, n_quarter), :], px2.at[k], x_dev[second])
        )
        x_at.append(base + x_half[second] * n_quarter)

    own_2 = reduce_2(own, ro1, ro2, own_1)

    cross = []
    for c in range(2):
        edge_2[c].wait_recv()
        edge[c, quarter_of(c), :] = edge[c, quarter_of(c), :] + re2[c]
        cross.append(sems.start(edge.at[c, quarter_of(c), :], arrive.at[c], t_right))

    for k in range(2):
        x_2[k].wait_recv()
        pgrad[rows(x_at[k], n_quarter), :] = pgrad[rows(x_at[k], n_quarter), :] + px2[k]

    n_z = 2 * n_quarter // NZ

    def z_rows(zz):
        return rows(x_at[0] + (zz // 4) * (x_at[1] - x_at[0]) + (zz % 4) * n_z, n_z)

    z_copies = []
    for k in range(1, NZ):
        z_copies.append(sems.start(pgrad.at[z_rows((z + k) % NZ), :], pz.at[k - 1], z_dev[k - 1]))

    gather_1 = []
    for c in range(2):
        own_2[c].wait_recv()
        cross[c].wait_recv()
        q = quarter_of(c)
        q8 = pl.ds(quarter_at(c) // 8, quarter_rows // 8)
        mine_now = obj_ref[c, q8].reshape(quarter_rows, SIDE)
        onew_ref[c, q, :] = mine_now + own[c, q, :] + ro2[c] + jnp.where(t == 0, 0.0, arrive[c])
        gather_1.append(sems.start(onew_ref.at[c, q, :], onew_ref.at[c, q, :], y_dev[order(c)[1]]))

    total = pgrad[z_rows(z), :]
    for k in range(1, NZ):
        z_copies[k - 1].wait_recv()
        total = total + pz[k - 1]
    pnew_ref[z_rows(z), :] = probe_ref[z_rows(z), :] + total * 0.5
    z_gather = []
    for k in range(1, NZ):
        z_gather.append(sems.start(pnew_ref.at[z_rows(z), :], pnew_ref.at[z_rows(z), :], z_dev[k - 1]))

    gather_2 = []
    for c in range(2):
        gather_1[c].wait_recv()
        q = rows(y_half[order(c)[0]] * half_rows, half_rows)
        gather_2.append(sems.start(onew_ref.at[c, q, :], onew_ref.at[c, q, :], y_dev[order(c)[0]]))

    for copy in z_gather:
        copy.wait_recv()
    x_g1, x_g2 = [], []
    for k in range(2):
        at = rows(x_at[k], n_quarter)
        x_g1.append(sems.start(pnew_ref.at[at, :], pnew_ref.at[at, :], x_dev[order(k)[1]]))
    for k in range(2):
        x_g1[k].wait_recv()
        at = rows(mine + k * n_part + x_half[order(k)[0]] * n_half, n_half)
        x_g2.append(sems.start(pnew_ref.at[at, :], pnew_ref.at[at, :], x_dev[order(k)[0]]))
    for k in range(2):
        x_g2[k].wait_recv()
    last = sems.start(pnew_ref.at[rows(mine, n_core), :], pnew_ref.at[rows(mine, n_core), :], peer)
    for c in range(2):
        gather_2[c].wait_recv()
    last.wait_recv()
    for copy in sems.started:
        copy.wait_send()


def on_device(object_tile, probe, amplitudes, row_offsets, col_offsets, scan_count):
    left, right = dft_blocks()
    vmem = pl.BlockSpec(memory_space=pltpu.VMEM)
    smem = pl.BlockSpec(memory_space=pltpu.SMEM)
    n = 2 * MODES * SIDE
    flat = probe.reshape(n, SIDE)
    places = jnp.stack(
        [
            *aligned(row_offsets),
            *aligned(ROWS - SIDE - row_offsets),
            (2 * SIDE - col_offsets) % (2 * SIDE),
            col_offsets,
        ]
    )
    active = (jnp.arange(SCANS, dtype=jnp.int32) < scan_count[0]).astype(F32)
    scratch = [
        pltpu.VMEM((2, ROWS // 8, 8, SIDE), F32),
        pltpu.VMEM((SCANS, 2, SIDE, SIDE), F32),
        pltpu.VMEM((2 * SIDE, SIDE), BF16),
        pltpu.VMEM((SIDE, 2 * SIDE), BF16),
        pltpu.VMEM((SCANS, MODES, SIDE, 2 * SIDE), BF16),
        pltpu.VMEM((SCANS, SIDE, SIDE), F32),
        pltpu.VMEM((SCANS, SIDE // 2, SIDE), F32),
        pltpu.VMEM((SCANS, SIDE // 4, SIDE), F32),
        pltpu.VMEM((SCANS, SIDE, SIDE), F32),
        pltpu.VMEM((SCANS, 2, 2 * SIDE // 8, 8, SIDE), F32),
        pltpu.VMEM((n, SIDE), F32),
        pltpu.VMEM((n // 2, SIDE), F32),
        pltpu.VMEM((2, n // 8, SIDE), F32),
        pltpu.VMEM((2, n // 16, SIDE), F32),
        pltpu.VMEM((NZ - 1, n // 64, SIDE), F32),
        pltpu.VMEM((2, ROWS, SIDE), F32),
        pltpu.VMEM((2, ROWS, SIDE), F32),
        pltpu.VMEM((2, ROWS // 2, SIDE), F32),
        pltpu.VMEM((2, ROWS // 4, SIDE), F32),
        pltpu.VMEM((2, ROWS // 2, SIDE), F32),
        pltpu.VMEM((2, ROWS // 4, SIDE), F32),
        pltpu.VMEM((2, ROWS // 4, SIDE), F32),
        pltpu.SemaphoreType.DMA((N_SEMS,)),
        pltpu.SemaphoreType.DMA((N_SEMS,)),
    ]
    object_new, probe_new = pl.pallas_call(
        kernel,
        out_shape=(
            jax.ShapeDtypeStruct(object_tile.shape, F32),
            jax.ShapeDtypeStruct(flat.shape, F32),
        ),
        in_specs=[smem, smem, vmem, vmem, vmem, vmem, vmem],
        out_specs=(vmem, vmem),
        scratch_shapes=scratch,
        compiler_params=pltpu.CompilerParams(
            collective_id=0, has_side_effects=True, vmem_limit_bytes=56 * 1024 * 1024
        ),
        cost_estimate=pl.CostEstimate(flops=3_300_000_000, bytes_accessed=6_000_000, transcendentals=131072),
    )(places, active, object_tile.reshape(2, ROWS // 8, 8, SIDE), flat, amplitudes, jnp.asarray(left), jnp.asarray(right))
    return object_new, probe_new.reshape(probe.shape)


def solution(mesh):
    in_specs = (
        P(None, None, "tile"),
        P("mode", None, None, None),
        P("tile", None, None),
        P("tile"),
        P("tile"),
        P("tile"),
    )
    out_specs = (P(None, None, "tile"), P("mode", None, None, None))
    return jax.shard_map(on_device, mesh=mesh, in_specs=in_specs, out_specs=out_specs, check_vma=False)
```

```python
import functools

import jax
import jax.numpy as jnp
import numpy as np
from jax import lax
from jax.experimental import pallas as pl
from jax.experimental.pallas import tpu as pltpu
from jax.sharding import PartitionSpec as P

SIDE = 256
ROWS = 384
MODES = 3
SCANS = 2
NX, NZ, NY = 4, 8, 4
N_TILE = 64
F32 = jnp.float32
BF16 = jnp.bfloat16
BLK = 32


def dft_blocks():
    counter = np.arange(SIDE)
    phase = (np.outer(counter, counter) % SIDE) * (2.0 * np.pi / SIDE)
    real = np.cos(phase) / np.sqrt(SIDE)
    imag = -np.sin(phase) / np.sqrt(SIDE)
    left = np.block([[real, -imag], [imag, real]])
    right = np.block([[real, imag], [-imag, real]])
    return left.astype(np.float32).astype(jnp.bfloat16), right.astype(np.float32).astype(jnp.bfloat16)


class Sems:
    def __init__(self, send, recv):
        self.send, self.recv, self.used, self.started = send, recv, 0, []

    def make(self, src, dst, dev):
        i = self.used
        self.used += 1
        copy = pltpu.make_async_remote_copy(
            src_ref=src,
            dst_ref=dst,
            send_sem=self.send.at[i],
            recv_sem=self.recv.at[i],
            device_id=dev,
            device_id_type=pl.DeviceIdType.MESH,
        )
        return copy

    def start(self, src, dst, dev):
        copy = self.make(src, dst, dev)
        copy.start()
        self.started.append(copy)
        return copy


N_SEMS = 64


def rows(start, size):
    return pl.ds(pl.multiple_of(start, 8), size)


def shifted(blocks, rest):
    turned = pltpu.roll(blocks, (16 - rest) % 8, axis=1)
    row = lax.broadcasted_iota(jnp.int32, turned[1:].shape, 1)
    return jnp.where(row < 8 - rest, turned[:-1], turned[1:])


def kernel(
    row_ref, col_ref, cnt_ref, obj_hbm, probe_hbm, amp_hbm, lf_hbm, rf_hbm,
    onew_ref, pnew_ref,
    obj, probe_ref, amp_ref, lf_ref, rf_ref,
    border, win, psi, half, spec, power, pw_a, pw_b, factor, pad, pgrad, p_core,
    px1, px2, pz, own, edge, ro1, ro2, re1, re2, arrive,
    send_sem, recv_sem, fetch_sem,
):
    t = lax.axis_index("tile")
    y = lax.axis_index("mode")
    core = t % 2
    z = (t // 2) % NZ
    x = t // (2 * NZ)
    sems = Sems(send_sem, recv_sem)

    def tile_dev(xx, zz, cc):
        return ((xx * NZ + zz) * 2 + cc, y)

    t_left = ((t + N_TILE - 1) % N_TILE, y)
    t_right = ((t + 1) % N_TILE, y)
    peer = tile_dev(x, z, 1 - core)

    def pairs(i):
        return (i + 1 - 2 * (i % 2), 3 - i, ((i + 1) // 2) % 2, i // 2)

    ya, yb, yha, yhb = pairs(y)
    xa, xb, xha, xhb = pairs(x)
    y_dev = ((t, ya), (t, yb))
    x_dev = (tile_dev(xa, z, core), tile_dev(xb, z, core))
    y_half = (yha, yhb)
    x_half = (xha, xhb)
    z_dev = [tile_dev(x, (z + k) % NZ, core) for k in range(1, NZ)]

    fetch = []
    for src, dst in ((obj_hbm, obj), (probe_hbm, probe_ref), (lf_hbm, lf_ref), (rf_hbm, rf_ref), (amp_hbm, amp_ref)):
        fetch.append(pltpu.make_async_copy(src, dst, fetch_sem.at[len(fetch)]))
        fetch[-1].start()

    barrier = pltpu.get_barrier_semaphore()
    partners = [t_left, t_right, *y_dev, *x_dev, *z_dev]
    for dev in partners:
        pl.semaphore_signal(barrier, inc=1, device_id=dev, device_id_type=pl.DeviceIdType.MESH)
    pl.semaphore_wait(barrier, len(partners))

    quarter_blocks = ROWS // 32

    def border_part(index):
        return pl.ds(index * quarter_blocks, quarter_blocks)

    def near(part, ref):
        return ref.at[:, border_part(part)]

    whole = sems.make(obj_hbm, border, peer)
    direct = [sems.make(near(k, obj_hbm), near(k, border), t_left) for k in (y, (y + 2) % NY)]
    passed = [sems.make(near(y, border), near(y, border), dev) for dev in y_dev]

    @pl.when(core == 1)
    def _():
        whole.start()

    @pl.when(core == 0)
    def _():
        direct[0].start()
        direct[1].start()

    for s in range(SCANS):
        for c in range(2):
            pad[s, c, 0:16] = jnp.zeros((16, 8, SIDE), F32)
            pad[s, c, 48:64] = jnp.zeros((16, 8, SIDE), F32)

    for copy in fetch:
        copy.wait()

    @pl.when(core == 1)
    def _():
        direct[0].wait_recv()
        passed[0].start()
        passed[1].start()
        direct[1].wait_recv()
        passed[0].wait_recv()
        passed[1].wait_recv()

    @pl.when(core == 0)
    def _():
        whole.wait_recv()

    lane = lax.broadcasted_iota(jnp.int32, (BLK // 8 + 1, 8, SIDE), 2)
    beyond = jnp.where(t == N_TILE - 1, 0.0, 1.0).astype(F32)

    def forward(s):
        top, col = row_ref[s], col_ref[s]
        base = jnp.minimum(top // 8, 15)
        rest = top - base * 8

        def cut(i, carry):
            at = pl.ds(base + i * (BLK // 8), BLK // 8 + 1)
            for c in range(2):
                block = jnp.where(lane >= col, obj[c, at], border[c, at] * beyond)
                block = pltpu.roll(shifted(block, rest), (SIDE - col) % SIDE, axis=2)
                win[s, c, rows(i * BLK, BLK), :] = block.reshape(BLK, SIDE)
            return carry

        lax.fori_loop(0, SIDE // BLK, cut, 0)

        def mode(m, carry):
            pr = probe_ref[rows(m * 2 * SIDE, SIDE), :]
            pi = probe_ref[rows(m * 2 * SIDE + SIDE, SIDE), :]
            wr, wi = win[s, 0], win[s, 1]
            psi[0:SIDE, :] = (pr * wr - pi * wi).astype(BF16)
            psi[SIDE:, :] = (pr * wi + pi * wr).astype(BF16)
            mid = jnp.dot(lf_ref[...], psi[...], preferred_element_type=F32).astype(BF16)
            half[:, 0:SIDE] = mid[0:SIDE]
            half[:, SIDE:] = mid[SIDE:]
            out = jnp.dot(half[...], rf_ref[...], preferred_element_type=F32).astype(BF16)
            spec[s, m] = out
            wide = out.astype(F32)
            wide = wide * wide
            power[s] = jnp.where(m == 0, 0.0, power[s]) + wide[:, :SIDE] + wide[:, SIDE:]
            return carry

        lax.fori_loop(0, MODES, mode, 0)

    def order(s):
        return (s, 1 - s)

    step1, step2 = [], []
    for s in range(SCANS):
        forward(s)
        first, _ = order(s)
        h = y_half[first]
        step1.append(sems.start(power.at[s, rows((1 - h) * 128, 128), :], pw_a.at[s], y_dev[first]))
    quarter = []
    for s in range(SCANS):
        first, second = order(s)
        h, g = y_half[first], y_half[second]
        base = h * 128
        step1[s].wait_recv()
        power[s, rows(base, 128), :] = power[s, rows(base, 128), :] + pw_a[s]
        step2.append(sems.start(power.at[s, rows(base + (1 - g) * 64, 64), :], pw_b.at[s], y_dev[second]))
        quarter.append(base + g * 64)
    gather1, gather2 = [], []
    for s in range(SCANS):
        first, second = order(s)
        q = rows(quarter[s], 64)
        step2[s].wait_recv()
        total = power[s, q, :] + pw_b[s]
        factor[s, q, :] = amp_ref[s, q, :] / jnp.maximum(jnp.sqrt(total), 0.5) - 1.0
        gather1.append(sems.start(factor.at[s, q, :], factor.at[s, q, :], y_dev[second]))
    for s in range(SCANS):
        first, second = order(s)
        q = rows(y_half[first] * 128, 128)
        gather1[s].wait_recv()
        gather2.append(sems.start(factor.at[s, q, :], factor.at[s, q, :], y_dev[first]))

    def backward(s):
        active = jnp.where(s < cnt_ref[0], 1.0, 0.0).astype(F32)

        def mode(m, carry):
            f = factor[s]
            psi[0:SIDE, :] = (spec[s, m, :, :SIDE].astype(F32) * f).astype(BF16)
            psi[SIDE:, :] = (spec[s, m, :, SIDE:].astype(F32) * f).astype(BF16)
            mid = jnp.dot(rf_ref[...], psi[...], preferred_element_type=F32).astype(BF16)
            half[:, 0:SIDE] = mid[0:SIDE]
            half[:, SIDE:] = mid[SIDE:]
            chi = jnp.dot(half[...], lf_ref[...], preferred_element_type=F32) * active
            cr, ci = chi[:, :SIDE], chi[:, SIDE:]
            at_r, at_i = rows(m * 2 * SIDE, SIDE), rows(m * 2 * SIDE + SIDE, SIDE)
            pr, pi = probe_ref[at_r, :], probe_ref[at_i, :]
            wr, wi = win[s, 0], win[s, 1]
            gr = (pr * cr + pi * ci).reshape(SIDE // 8, 8, SIDE)
            gi = (pr * ci - pi * cr).reshape(SIDE // 8, 8, SIDE)
            pad[s, 0, 16:48] = jnp.where(m == 0, 0.0, pad[s, 0, 16:48]) + gr
            pad[s, 1, 16:48] = jnp.where(m == 0, 0.0, pad[s, 1, 16:48]) + gi
            if s == 0:
                pgrad[at_r, :] = wr * cr + wi * ci
                pgrad[at_i, :] = wr * ci - wi * cr
            else:
                pgrad[at_r, :] = pgrad[at_r, :] + wr * cr + wi * ci
                pgrad[at_i, :] = pgrad[at_i, :] + wr * ci - wi * cr
            return carry

        lax.fori_loop(0, MODES, mode, 0)

    for s in range(SCANS):
        gather2[s].wait_recv()
        backward(s)

    n_core = MODES * SIDE
    mine = core * n_core
    core_copy = sems.start(pgrad.at[rows((1 - core) * n_core, n_core), :], p_core, peer)

    def place(i, carry):
        for c in range(2):
            inside = outside = 0.0
            for s in range(SCANS):
                col, down = col_ref[s], 128 - row_ref[s]
                base = jnp.minimum(down // 8, 15)
                block = pad[s, c, pl.ds(base + i * (BLK // 8), BLK // 8 + 1)]
                block = pltpu.roll(shifted(block, down - base * 8), col, axis=2)
                here = lane[1:] >= col
                inside = inside + jnp.where(here, block, 0.0)
                outside = outside + jnp.where(here, 0.0, block)
            own[c, rows(i * BLK, BLK), :] = inside.reshape(BLK, SIDE)
            edge[c, rows(i * BLK, BLK), :] = outside.reshape(BLK, SIDE)
        return carry

    lax.fori_loop(0, ROWS // BLK, place, 0)

    half_rows, quarter_rows = ROWS // 2, ROWS // 4

    def reduce_1(grid, landing):
        copies = []
        for c in range(2):
            h = y_half[order(c)[0]]
            copies.append(
                sems.start(grid.at[c, rows((1 - h) * half_rows, half_rows), :], landing.at[c], y_dev[order(c)[0]])
            )
        return copies

    def reduce_2(grid, landing_1, landing_2, copies):
        result = []
        for c in range(2):
            first, second = order(c)
            h, g = y_half[first], y_half[second]
            base = h * half_rows
            copies[c].wait_recv()
            grid[c, rows(base, half_rows), :] = grid[c, rows(base, half_rows), :] + landing_1[c]
            result.append(
                sems.start(
                    grid.at[c, rows(base + (1 - g) * quarter_rows, quarter_rows), :], landing_2.at[c], y_dev[second]
                )
            )
        return result

    def quarter_at(c):
        first, second = order(c)
        return y_half[first] * half_rows + y_half[second] * quarter_rows

    def quarter_of(c):
        return rows(quarter_at(c), quarter_rows)

    edge_1 = reduce_1(edge, re1)
    own_1 = reduce_1(own, ro1)

    core_copy.wait_recv()
    pgrad[rows(mine, n_core), :] = pgrad[rows(mine, n_core), :] + p_core[...]
    n_part, n_half, n_quarter = n_core // 2, n_core // 4, n_core // 8
    x_1 = []
    for k in range(2):
        first, _ = order(k)
        x_1.append(
            sems.start(
                pgrad.at[rows(mine + k * n_part + (1 - x_half[first]) * n_half, n_half), :], px1.at[k], x_dev[first]
            )
        )

    edge_2 = reduce_2(edge, re1, re2, edge_1)

    x_2, x_at = [], []
    for k in range(2):
        first, second = order(k)
        base = mine + k * n_part + x_half[first] * n_half
        x_1[k].wait_recv()
        pgrad[rows(base, n_half), :] = pgrad[rows(base, n_half), :] + px1[k]
        x_2.append(
            sems.start(pgrad.at[rows(base + (1 - x_half[second]) * n_quarter, n_quarter), :], px2.at[k], x_dev[second])
        )
        x_at.append(base + x_half[second] * n_quarter)

    own_2 = reduce_2(own, ro1, ro2, own_1)

    cross = []
    for c in range(2):
        edge_2[c].wait_recv()
        edge[c, quarter_of(c), :] = edge[c, quarter_of(c), :] + re2[c]
        cross.append(sems.start(edge.at[c, quarter_of(c), :], arrive.at[c], t_right))

    for k in range(2):
        x_2[k].wait_recv()
        pgrad[rows(x_at[k], n_quarter), :] = pgrad[rows(x_at[k], n_quarter), :] + px2[k]

    n_z = 2 * n_quarter // NZ

    def z_rows(zz):
        return rows(x_at[0] + (zz // 4) * (x_at[1] - x_at[0]) + (zz % 4) * n_z, n_z)

    z_copies = []
    for k in range(1, NZ):
        z_copies.append(sems.start(pgrad.at[z_rows((z + k) % NZ), :], pz.at[k - 1], z_dev[k - 1]))

    gather_1 = []
    for c in range(2):
        own_2[c].wait_recv()
        cross[c].wait_recv()
        q = quarter_of(c)
        q8 = pl.ds(quarter_at(c) // 8, quarter_rows // 8)
        mine_now = obj[c, q8].reshape(quarter_rows, SIDE)
        onew_ref[c, q, :] = mine_now + own[c, q, :] + ro2[c] + jnp.where(t == 0, 0.0, arrive[c])
        gather_1.append(sems.start(onew_ref.at[c, q, :], onew_ref.at[c, q, :], y_dev[order(c)[1]]))

    total = pgrad[z_rows(z), :]
    for k in range(1, NZ):
        z_copies[k - 1].wait_recv()
        total = total + pz[k - 1]
    pnew_ref[z_rows(z), :] = probe_ref[z_rows(z), :] + total * 0.5
    z_gather = []
    for k in range(1, NZ):
        z_gather.append(sems.start(pnew_ref.at[z_rows(z), :], pnew_ref.at[z_rows(z), :], z_dev[k - 1]))

    gather_2 = []
    for c in range(2):
        gather_1[c].wait_recv()
        q = rows(y_half[order(c)[0]] * half_rows, half_rows)
        gather_2.append(sems.start(onew_ref.at[c, q, :], onew_ref.at[c, q, :], y_dev[order(c)[0]]))

    for copy in z_gather:
        copy.wait_recv()
    x_g1, x_g2 = [], []
    for k in range(2):
        at = rows(x_at[k], n_quarter)
        x_g1.append(sems.start(pnew_ref.at[at, :], pnew_ref.at[at, :], x_dev[order(k)[1]]))
    for k in range(2):
        x_g1[k].wait_recv()
        at = rows(mine + k * n_part + x_half[order(k)[0]] * n_half, n_half)
        x_g2.append(sems.start(pnew_ref.at[at, :], pnew_ref.at[at, :], x_dev[order(k)[0]]))
    for k in range(2):
        x_g2[k].wait_recv()
    last = sems.start(pnew_ref.at[rows(mine, n_core), :], pnew_ref.at[rows(mine, n_core), :], peer)
    for c in range(2):
        gather_2[c].wait_recv()
    last.wait_recv()
    for copy in sems.started:
        copy.wait_send()

    @pl.when(core == 1)
    def _():
        for copy in (whole, *passed):
            copy.wait_send()

    @pl.when(core == 0)
    def _():
        for copy in direct:
            copy.wait_send()


def on_device(object_tile, probe, amplitudes, row_offsets, col_offsets, scan_count):
    left, right = dft_blocks()
    vmem = pl.BlockSpec(memory_space=pltpu.VMEM)
    smem = pl.BlockSpec(memory_space=pltpu.SMEM)
    n = 2 * MODES * SIDE
    flat = probe.reshape(n, SIDE)
    anywhere = pl.BlockSpec(memory_space=pl.ANY)
    scratch = [
        pltpu.VMEM((2, ROWS // 8, 8, SIDE), F32),
        pltpu.VMEM((n, SIDE), F32),
        pltpu.VMEM((SCANS, SIDE, SIDE), F32),
        pltpu.VMEM((2 * SIDE, 2 * SIDE), BF16),
        pltpu.VMEM((2 * SIDE, 2 * SIDE), BF16),
        pltpu.VMEM((2, ROWS // 8, 8, SIDE), F32),
        pltpu.VMEM((SCANS, 2, SIDE, SIDE), F32),
        pltpu.VMEM((2 * SIDE, SIDE), BF16),
        pltpu.VMEM((SIDE, 2 * SIDE), BF16),
        pltpu.VMEM((SCANS, MODES, SIDE, 2 * SIDE), BF16),
        pltpu.VMEM((SCANS, SIDE, SIDE), F32),
        pltpu.VMEM((SCANS, SIDE // 2, SIDE), F32),
        pltpu.VMEM((SCANS, SIDE // 4, SIDE), F32),
        pltpu.VMEM((SCANS, SIDE, SIDE), F32),
        pltpu.VMEM((SCANS, 2, 2 * SIDE // 8, 8, SIDE), F32),
        pltpu.VMEM((n, SIDE), F32),
        pltpu.VMEM((n // 2, SIDE), F32),
        pltpu.VMEM((2, n // 8, SIDE), F32),
        pltpu.VMEM((2, n // 16, SIDE), F32),
        pltpu.VMEM((NZ - 1, n // 64, SIDE), F32),
        pltpu.VMEM((2, ROWS, SIDE), F32),
        pltpu.VMEM((2, ROWS, SIDE), F32),
        pltpu.VMEM((2, ROWS // 2, SIDE), F32),
        pltpu.VMEM((2, ROWS // 4, SIDE), F32),
        pltpu.VMEM((2, ROWS // 2, SIDE), F32),
        pltpu.VMEM((2, ROWS // 4, SIDE), F32),
        pltpu.VMEM((2, ROWS // 4, SIDE), F32),
        pltpu.SemaphoreType.DMA((N_SEMS,)),
        pltpu.SemaphoreType.DMA((N_SEMS,)),
        pltpu.SemaphoreType.DMA((5,)),
    ]
    object_new, probe_new = pl.pallas_call(
        kernel,
        out_shape=(
            jax.ShapeDtypeStruct(object_tile.shape, F32),
            jax.ShapeDtypeStruct(flat.shape, F32),
        ),
        in_specs=[smem] * 3 + [anywhere] * 5,
        out_specs=(vmem, vmem),
        scratch_shapes=scratch,
        compiler_params=pltpu.CompilerParams(
            collective_id=0, has_side_effects=True, vmem_limit_bytes=56 * 1024 * 1024
        ),
        cost_estimate=pl.CostEstimate(flops=3_300_000_000, bytes_accessed=6_000_000, transcendentals=131072),
    )(
        row_offsets,
        col_offsets,
        scan_count,
        object_tile.reshape(2, ROWS // 8, 8, SIDE),
        flat,
        amplitudes,
        jnp.asarray(left),
        jnp.asarray(right),
    )
    return object_new, probe_new.reshape(probe.shape)


def solution(mesh):
    in_specs = (
        P(None, None, "tile"),
        P("mode", None, None, None),
        P("tile", None, None),
        P("tile"),
        P("tile"),
        P("tile"),
    )
    out_specs = (P(None, None, "tile"), P("mode", None, None, None))
    return jax.shard_map(on_device, mesh=mesh, in_specs=in_specs, out_specs=out_specs, check_vma=False)
```

```python
import functools

import jax
import jax.numpy as jnp
import numpy as np
from jax import lax
from jax.experimental import pallas as pl
from jax.experimental.pallas import tpu as pltpu
from jax.sharding import PartitionSpec as P

SIDE = 256
ROWS = 384
MODES = 3
SCANS = 2
NX, NZ, NY = 4, 8, 4
N_TILE = 64
F32 = jnp.float32
BF16 = jnp.bfloat16
BLK = 32


def dft_blocks():
    counter = np.arange(SIDE)
    phase = (np.outer(counter, counter) % SIDE) * (2.0 * np.pi / SIDE)
    real = np.cos(phase) / np.sqrt(SIDE)
    imag = -np.sin(phase) / np.sqrt(SIDE)
    left = np.block([[real, -imag], [imag, real]])
    right = np.block([[real, imag], [-imag, real]])
    return left.astype(np.float32).astype(jnp.bfloat16), right.astype(np.float32).astype(jnp.bfloat16)


class Sems:
    def __init__(self, send, recv):
        self.send, self.recv, self.used, self.started = send, recv, 0, []

    def make(self, src, dst, dev):
        i = self.used
        self.used += 1
        copy = pltpu.make_async_remote_copy(
            src_ref=src,
            dst_ref=dst,
            send_sem=self.send.at[i],
            recv_sem=self.recv.at[i],
            device_id=dev,
            device_id_type=pl.DeviceIdType.MESH,
        )
        return copy

    def start(self, src, dst, dev):
        copy = self.make(src, dst, dev)
        copy.start()
        self.started.append(copy)
        return copy


N_SEMS = 128
Z_ORDER = (4, 3, 5, 2, 6, 1, 7, 0)


def rows(start, size):
    return pl.ds(pl.multiple_of(start, 8), size)


def shifted(blocks, rest):
    turned = pltpu.roll(blocks, (16 - rest) % 8, axis=1)
    row = lax.broadcasted_iota(jnp.int32, turned[1:].shape, 1)
    return jnp.where(row < 8 - rest, turned[:-1], turned[1:])


def kernel(
    row_ref, col_ref, cnt_ref, obj_hbm, probe_hbm, amp_hbm, lf_hbm, rf_hbm,
    onew_ref, pnew_ref,
    obj, probe_ref, amp_ref, lf_ref, rf_ref,
    border, win, psi, half, spec, power, pw, factor, pad, pgrad, p_core,
    px, pz, own, edge, from_core, ro, re, arrive,
    send_sem, recv_sem, fetch_sem,
):
    t = lax.axis_index("tile")
    y = lax.axis_index("mode")
    core = t % 2
    z = (t // 2) % NZ
    x = t // (2 * NZ)
    sems = Sems(send_sem, recv_sem)

    def tile_dev(xx, zz, cc):
        return ((xx * NZ + zz) * 2 + cc, y)

    t_left = ((t + N_TILE - 1) % N_TILE, y)
    t_right = ((t + 1) % N_TILE, y)
    peer = tile_dev(x, z, 1 - core)

    y_on = [(t, (y + k) % NY) for k in range(1, NY)]
    x_on = [tile_dev((x + k) % NX, z, core) for k in range(1, NX)]
    z_dev = [tile_dev(x, (z + k) % NZ, core) for k in range(1, NZ)]

    fetch = []
    for src, dst in ((obj_hbm, obj), (probe_hbm, probe_ref), (lf_hbm, lf_ref), (rf_hbm, rf_ref), (amp_hbm, amp_ref)):
        fetch.append(pltpu.make_async_copy(src, dst, fetch_sem.at[len(fetch)]))
        fetch[-1].start()

    barrier = pltpu.get_barrier_semaphore()
    partners = [t_left, t_right, *y_on, *x_on, *z_dev]
    for dev in partners:
        pl.semaphore_signal(barrier, inc=1, device_id=dev, device_id_type=pl.DeviceIdType.MESH)
    pl.semaphore_wait(barrier, len(partners))

    def blocks(index, first, last):
        return pl.ds(index * (ROWS // 32) + first, last - first)

    def near(ref, at):
        return ref.at[:, at]

    y_up, y_across, y_down = [(y + k) % NY for k in range(1, NY)]
    whole = sems.make(obj_hbm, border, peer)
    ranges = (blocks(y, 0, 8), blocks(y_across, 0, 12), blocks(y, 8, 12), blocks(y_up, 8, 12), blocks(y_down, 8, 12))
    direct = [sems.make(near(obj_hbm, at), near(border, at), t_left) for at in ranges]
    passed = [sems.make(near(border, ranges[0]), near(border, ranges[0]), dev) for dev in (y_on[0], y_on[2])]

    @pl.when(core == 1)
    def _():
        whole.start()

    @pl.when(core == 0)
    def _():
        for copy in direct:
            copy.start()

    for s in range(SCANS):
        for c in range(2):
            pad[s, c, 0:16] = jnp.zeros((16, 8, SIDE), F32)
            pad[s, c, 48:64] = jnp.zeros((16, 8, SIDE), F32)

    for copy in fetch:
        copy.wait()

    @pl.when(core == 1)
    def _():
        direct[0].wait_recv()
        passed[0].start()
        passed[1].start()
        for copy in (*direct[1:], *passed):
            copy.wait_recv()

    @pl.when(core == 0)
    def _():
        whole.wait_recv()

    lane = lax.broadcasted_iota(jnp.int32, (BLK // 8 + 1, 8, SIDE), 2)
    beyond = jnp.where(t == N_TILE - 1, 0.0, 1.0).astype(F32)

    def forward(s):
        top, col = row_ref[s], col_ref[s]
        base = jnp.minimum(top // 8, 15)
        rest = top - base * 8

        def cut(i, carry):
            at = pl.ds(base + i * (BLK // 8), BLK // 8 + 1)
            for c in range(2):
                block = jnp.where(lane >= col, obj[c, at], border[c, at] * beyond)
                block = pltpu.roll(shifted(block, rest), (SIDE - col) % SIDE, axis=2)
                win[s, c, rows(i * BLK, BLK), :] = block.reshape(BLK, SIDE)
            return carry

        lax.fori_loop(0, SIDE // BLK, cut, 0)

        def mode(m):
            pr, pi = probe_ref[m, :SIDE], probe_ref[m, SIDE:]
            wr, wi = win[s, 0], win[s, 1]
            psi[m, 0:SIDE, :] = (pr * wr - pi * wi).astype(BF16)
            psi[m, SIDE:, :] = (pr * wi + pi * wr).astype(BF16)
            mid = jnp.dot(lf_ref[...], psi[m], preferred_element_type=F32).astype(BF16)
            half[m, :, 0:SIDE] = mid[0:SIDE]
            half[m, :, SIDE:] = mid[SIDE:]
            out = jnp.dot(half[m], rf_ref[...], preferred_element_type=F32).astype(BF16)
            spec[s, m] = out
            wide = out.astype(F32)
            wide = wide * wide
            wide = wide[:, :SIDE] + wide[:, SIDE:]
            power[s] = wide if m == 0 else power[s] + wide

        for m in range(MODES):
            mode(m)

    n_q = SIDE // NY

    def q_rows(index):
        return rows(index * n_q, n_q)

    sums = []
    for s in range(SCANS):
        forward(s)
        sums.append([])
        for k in (2, 1, 3):
            src = power.at[s, q_rows((y + k) % NY), :]
            sums[s].append(sems.start(src, pw.at[s, k - 1], y_on[k - 1]))
    gathers = []
    for s in range(SCANS):
        for copy in sums[s]:
            copy.wait_recv()
        q = q_rows(y)
        total = power[s, q, :] + pw[s, 0] + pw[s, 1] + pw[s, 2]
        factor[s, q, :] = amp_ref[s, q, :] / jnp.maximum(jnp.sqrt(total), 0.5) - 1.0
        gathers.append([sems.start(factor.at[s, q, :], factor.at[s, q, :], y_on[k - 1]) for k in (2, 1, 3)])

    def backward(s):
        active = jnp.where(s < cnt_ref[0], 1.0, 0.0).astype(F32)

        def mode(m):
            f = factor[s]
            psi[m, 0:SIDE, :] = (spec[s, m, :, :SIDE].astype(F32) * f).astype(BF16)
            psi[m, SIDE:, :] = (spec[s, m, :, SIDE:].astype(F32) * f).astype(BF16)
            mid = jnp.dot(rf_ref[...], psi[m], preferred_element_type=F32).astype(BF16)
            half[m, :, 0:SIDE] = mid[0:SIDE]
            half[m, :, SIDE:] = mid[SIDE:]
            chi = jnp.dot(half[m], lf_ref[...], preferred_element_type=F32) * active
            cr, ci = chi[:, :SIDE], chi[:, SIDE:]
            pr, pi = probe_ref[m, :SIDE], probe_ref[m, SIDE:]
            wr, wi = win[s, 0], win[s, 1]
            gr = (pr * cr + pi * ci).reshape(SIDE // 8, 8, SIDE)
            gi = (pr * ci - pi * cr).reshape(SIDE // 8, 8, SIDE)
            pad[s, 0, 16:48] = gr if m == 0 else pad[s, 0, 16:48] + gr
            pad[s, 1, 16:48] = gi if m == 0 else pad[s, 1, 16:48] + gi
            pgr = wr * cr + wi * ci
            pgi = wr * ci - wi * cr
            if s == 0:
                pgrad[m, :SIDE] = pgr
                pgrad[m, SIDE:] = pgi
            else:
                pgrad[m, :SIDE] = pgrad[m, :SIDE] + pgr
                pgrad[m, SIDE:] = pgrad[m, SIDE:] + pgi

        return mode

    def part(index):
        return rows(index * SIDE, SIDE)

    core_sum = []
    for s in range(SCANS):
        for copy in gathers[s]:
            copy.wait_recv()
        mode = backward(s)
        for m in range(MODES):
            mode(m)
            if s == SCANS - 1:
                core_sum.append(sems.start(pgrad.at[m, part(1 - core), :], p_core.at[m], peer))

    def place(i, carry):
        for c in range(2):
            inside = outside = 0.0
            for s in range(SCANS):
                col, down = col_ref[s], 128 - row_ref[s]
                base = jnp.minimum(down // 8, 15)
                block = pad[s, c, pl.ds(base + i * (BLK // 8), BLK // 8 + 1)]
                block = pltpu.roll(shifted(block, down - base * 8), col, axis=2)
                here = lane[1:] >= col
                inside = inside + jnp.where(here, block, 0.0)
                outside = outside + jnp.where(here, 0.0, block)
            own[c, rows(i * BLK, BLK), :] = inside.reshape(BLK, SIDE)
            edge[c, rows(i * BLK, BLK), :] = outside.reshape(BLK, SIDE)
        return carry

    lax.fori_loop(0, ROWS // BLK, place, 0)

    quarter_rows = ROWS // NY

    def quarter(index):
        return rows(index * quarter_rows, quarter_rows)

    def object_flow():
        core_edge = sems.make(edge, from_core, peer)
        far = (2, 1, 3)
        edge_sum = [sems.make(edge.at[:, quarter((y + k) % NY), :], re.at[k - 1], y_on[k - 1]) for k in far]
        cross = sems.make(edge.at[:, quarter(y), :], arrive, t_right)

        @pl.when(core == 0)
        def _():
            core_edge.start()

        @pl.when(core == 1)
        def _():
            for copy in edge_sum:
                copy.start()

        yield 3.5

        @pl.when(core == 0)
        def _():
            core_edge.wait_send()

        @pl.when(core == 1)
        def _():
            core_edge.wait_recv()
            own[...] = own[...] + from_core[...]

        own_sum = []
        for c in range(2):
            for k in far:
                src = own.at[c, quarter((y + k) % NY), :]
                own_sum.append(sems.start(src, ro.at[k - 1, c], y_on[k - 1]))
        yield 8.0

        @pl.when(core == 1)
        def _():
            for copy in edge_sum:
                copy.wait_recv()
            edge[:, quarter(y), :] = edge[:, quarter(y), :] + re[0] + re[1] + re[2]
            cross.start()

        yield 14.8

        @pl.when(core == 0)
        def _():
            cross.wait_recv()

        @pl.when((core == 1) | (t == 0))
        def _():
            arrive[...] = jnp.zeros(arrive.shape, F32)

        q8 = pl.ds(y * (quarter_rows // 8), quarter_rows // 8)
        spread = []
        for c in range(2):
            for copy in own_sum[3 * c : 3 * c + 3]:
                copy.wait_recv()
            total = own[c, quarter(y), :] + ro[0, c] + ro[1, c] + ro[2, c] + arrive[c]
            onew_ref[c, quarter(y), :] = obj[c, q8].reshape(quarter_rows, SIDE) + total
            here = onew_ref.at[c, quarter(y), :]
            spread += [sems.start(here, here, y_on[k - 1]) for k in far]
        yield 27.0
        for copy in spread:
            copy.wait_recv()

        @pl.when(core == 1)
        def _():
            for copy in (*edge_sum, cross):
                copy.wait_send()

    def piece(xx, zz):
        return rows(core * SIDE + (xx * NZ + zz) * 8, 8)

    def group(xx):
        return rows(core * SIDE + xx * NZ * 8, NZ * 8)

    def same(xx, zz):
        return pnew_ref.at[:, piece(xx, zz), :]

    def probe_flow():
        yield 1.5
        for m in range(MODES):
            core_sum[m].wait_recv()
            pgrad[m, part(core), :] = pgrad[m, part(core), :] + p_core[m]
        x_sum = {}
        for k in Z_ORDER:
            for d in (2, 1, 3):
                src = pgrad.at[:, piece((x + d) % NX, (z + k) % NZ), :]
                x_sum[k, d] = sems.start(src, px.at[k, d - 1], x_on[d - 1])
        z_sum = {}
        for j, k in enumerate(Z_ORDER):
            yield 5.8 + 0.92 * j
            for d in (2, 1, 3):
                x_sum[k, d].wait_recv()
            at = piece(x, (z + k) % NZ)
            pgrad[:, at, :] = pgrad[:, at, :] + px[k, 0] + px[k, 1] + px[k, 2]
            if k:
                z_sum[k] = sems.start(pgrad.at[:, at, :], pz.at[k - 1], z_dev[k - 1])
        yield 14.5
        here = piece(x, z)
        total = pgrad[:, here, :]
        for k in Z_ORDER[:-1]:
            z_sum[k].wait_recv()
            total = total + pz[k - 1]
        pnew_ref[:, here, :] = probe_ref[:, here, :] + total * 0.5
        z_all = {k: sems.start(same(x, z), same(x, z), z_dev[k - 1]) for k in Z_ORDER[:-1]}
        x_all = {}
        for j, k in enumerate(Z_ORDER[::-1]):
            zz = (z + NZ - k) % NZ
            if k:
                yield 17.0 + 0.5 * j
                z_all[k].wait_recv()
            for d in (2, 1, 3):
                x_all[k, d] = sems.start(same(x, zz), same(x, zz), x_on[d - 1])
        core_all = [sems.start(pnew_ref.at[:, group(x), :], pnew_ref.at[:, group(x), :], peer)]
        yield 26.0
        for d in (1, 3, 2):
            for k in Z_ORDER:
                x_all[k, d].wait_recv()
            at = group((x + NX - d) % NX)
            core_all.append(sems.start(pnew_ref.at[:, at, :], pnew_ref.at[:, at, :], peer))
        yield 28.0
        for copy in core_all:
            copy.wait_recv()

    flows = [object_flow(), probe_flow()]
    due = [next(flow) for flow in flows]
    while flows:
        i = due.index(min(due))
        at = next(flows[i], None)
        if at is None:
            del flows[i], due[i]
        else:
            due[i] = at

    for copy in sems.started:
        copy.wait_send()

    @pl.when(core == 1)
    def _():
        for copy in (whole, *passed):
            copy.wait_send()

    @pl.when(core == 0)
    def _():
        for copy in direct:
            copy.wait_send()


def on_device(object_tile, probe, amplitudes, row_offsets, col_offsets, scan_count):
    left, right = dft_blocks()
    vmem = pl.BlockSpec(memory_space=pltpu.VMEM)
    smem = pl.BlockSpec(memory_space=pltpu.SMEM)
    stacked = (MODES, 2 * SIDE, SIDE)
    anywhere = pl.BlockSpec(memory_space=pl.ANY)
    scratch = [
        pltpu.VMEM((2, ROWS // 8, 8, SIDE), F32),
        pltpu.VMEM(stacked, F32),
        pltpu.VMEM((SCANS, SIDE, SIDE), F32),
        pltpu.VMEM((2 * SIDE, 2 * SIDE), BF16),
        pltpu.VMEM((2 * SIDE, 2 * SIDE), BF16),
        pltpu.VMEM((2, ROWS // 8, 8, SIDE), F32),
        pltpu.VMEM((SCANS, 2, SIDE, SIDE), F32),
        pltpu.VMEM((MODES, 2 * SIDE, SIDE), BF16),
        pltpu.VMEM((MODES, SIDE, 2 * SIDE), BF16),
        pltpu.VMEM((SCANS, MODES, SIDE, 2 * SIDE), BF16),
        pltpu.VMEM((SCANS, SIDE, SIDE), F32),
        pltpu.VMEM((SCANS, NY - 1, SIDE // NY, SIDE), F32),
        pltpu.VMEM((SCANS, SIDE, SIDE), F32),
        pltpu.VMEM((SCANS, 2, 2 * SIDE // 8, 8, SIDE), F32),
        pltpu.VMEM(stacked, F32),
        pltpu.VMEM((MODES, SIDE, SIDE), F32),
        pltpu.VMEM((NZ, NX - 1, MODES, 8, SIDE), F32),
        pltpu.VMEM((NZ - 1, MODES, 8, SIDE), F32),
        pltpu.VMEM((2, ROWS, SIDE), F32),
        pltpu.VMEM((2, ROWS, SIDE), F32),
        pltpu.VMEM((2, ROWS, SIDE), F32),
        pltpu.VMEM((NY - 1, 2, ROWS // NY, SIDE), F32),
        pltpu.VMEM((NY - 1, 2, ROWS // NY, SIDE), F32),
        pltpu.VMEM((2, ROWS // 4, SIDE), F32),
        pltpu.SemaphoreType.DMA((N_SEMS,)),
        pltpu.SemaphoreType.DMA((N_SEMS,)),
        pltpu.SemaphoreType.DMA((5,)),
    ]
    object_new, probe_new = pl.pallas_call(
        kernel,
        out_shape=(
            pltpu.VMEM(object_tile.shape, F32),
            pltpu.VMEM(stacked, F32),
        ),
        in_specs=[smem] * 3 + [anywhere] * 5,
        out_specs=(vmem, vmem),
        scratch_shapes=scratch,
        compiler_params=pltpu.CompilerParams(
            collective_id=0, has_side_effects=True, vmem_limit_bytes=56 * 1024 * 1024
        ),
        cost_estimate=pl.CostEstimate(flops=3_300_000_000, bytes_accessed=6_000_000, transcendentals=131072),
    )(
        row_offsets,
        col_offsets,
        scan_count,
        object_tile.reshape(2, ROWS // 8, 8, SIDE),
        probe.reshape(stacked),
        amplitudes,
        jnp.asarray(left),
        jnp.asarray(right),
    )
    return object_new, probe_new.reshape(probe.shape)


def solution(mesh):
    in_specs = (
        P(None, None, "tile"),
        P("mode", None, None, None),
        P("tile", None, None),
        P("tile"),
        P("tile"),
        P("tile"),
    )
    out_specs = (P(None, None, "tile"), P("mode", None, None, None))
    return jax.shard_map(on_device, mesh=mesh, in_specs=in_specs, out_specs=out_specs, check_vma=False)
```

```python
import functools

import jax
import jax.numpy as jnp
import numpy as np
from jax import lax
from jax.experimental import pallas as pl
from jax.experimental.pallas import tpu as pltpu
from jax.sharding import PartitionSpec as P

SIDE = 256
ROWS = 384
MODES = 3
SCANS = 2
NX, NZ, NY = 4, 8, 4
N_TILE = 64
F32 = jnp.float32
BF16 = jnp.bfloat16
BLK = 32


def dft_blocks():
    counter = np.arange(SIDE)
    phase = (np.outer(counter, counter) % SIDE) * (2.0 * np.pi / SIDE)
    real = np.cos(phase) / np.sqrt(SIDE)
    imag = -np.sin(phase) / np.sqrt(SIDE)
    left = np.block([[real, -imag], [imag, real]])
    right = np.block([[real, imag], [-imag, real]])
    return left.astype(np.float32).astype(jnp.bfloat16), right.astype(np.float32).astype(jnp.bfloat16)


class Sems:
    def __init__(self, send, recv):
        self.send, self.recv, self.used, self.started = send, recv, 0, []

    def make(self, src, dst, dev):
        i = self.used
        self.used += 1
        copy = pltpu.make_async_remote_copy(
            src_ref=src,
            dst_ref=dst,
            send_sem=self.send.at[i],
            recv_sem=self.recv.at[i],
            device_id=dev,
            device_id_type=pl.DeviceIdType.MESH,
        )
        return copy

    def start(self, src, dst, dev):
        copy = self.make(src, dst, dev)
        copy.start()
        self.started.append(copy)
        return copy


N_SEMS = 288
Z_ORDER = (4, 3, 5, 2, 6, 1, 7, 0)


def rows(start, size):
    return pl.ds(pl.multiple_of(start, 8), size)


def shifted(blocks, rest):
    turned = pltpu.roll(blocks, (16 - rest) % 8, axis=1)
    row = lax.broadcasted_iota(jnp.int32, turned[1:].shape, 1)
    return jnp.where(row < 8 - rest, turned[:-1], turned[1:])


def kernel(
    row_ref, col_ref, cnt_ref, obj_hbm, probe_hbm, amp_hbm, lf_hbm, rf_hbm,
    onew_ref, pnew_ref,
    obj, probe_ref, amp_ref, lf_ref, rf_ref,
    border, win, psi, half, spec, power, pw, factor, pad, pgrad, p_core,
    px, pz, own, edge, from_core, ro, re, arrive,
    send_sem, recv_sem, fetch_sem, known,
):
    t = lax.axis_index("tile")
    y = lax.axis_index("mode")
    core = t % 2
    z = (t // 2) % NZ
    x = t // (2 * NZ)
    sems = Sems(send_sem, recv_sem)

    def tile_dev(xx, zz, cc):
        return ((xx * NZ + zz) * 2 + cc, y)

    t_left = ((t + N_TILE - 1) % N_TILE, y)
    t_right = ((t + 1) % N_TILE, y)
    peer = tile_dev(x, z, 1 - core)

    y_on = [(t, (y + k) % NY) for k in range(1, NY)]
    x_on = [tile_dev((x + k) % NX, z, core) for k in range(1, NX)]
    z_dev = [tile_dev(x, (z + k) % NZ, core) for k in range(1, NZ)]

    fetch = []
    for src, dst in ((obj_hbm, obj), (probe_hbm, probe_ref), (lf_hbm, lf_ref), (rf_hbm, rf_ref), (amp_hbm, amp_ref)):
        fetch.append(pltpu.make_async_copy(src, dst, fetch_sem.at[len(fetch)]))
        fetch[-1].start()

    def tell(semaphore, devices):
        for dev in devices:
            pl.semaphore_signal(semaphore, inc=1, device_id=dev, device_id_type=pl.DeviceIdType.MESH)

    barrier = pltpu.get_barrier_semaphore()
    z_next = [z_dev[0], z_dev[-1]]
    near_by = [y_on[0], y_on[2], x_on[0], x_on[2], *z_next]
    tell(barrier, [t_left, t_right, *near_by])
    pl.semaphore_wait(barrier, 2 + len(near_by))
    tell(known.at[0], near_by)

    def blocks(index, first, last):
        return pl.ds(index * (ROWS // 32) + first, last - first)

    def near(ref, at):
        return ref.at[:, at]

    y_up, y_across, y_down = [(y + k) % NY for k in range(1, NY)]
    whole = sems.make(obj_hbm, border, peer)
    ranges = (blocks(y, 0, 8), blocks(y_across, 0, 12), blocks(y, 8, 12), blocks(y_up, 8, 12), blocks(y_down, 8, 12))
    direct = [sems.make(near(obj_hbm, at), near(border, at), t_left) for at in ranges]
    passed = [sems.make(near(border, ranges[0]), near(border, ranges[0]), dev) for dev in (y_on[0], y_on[2])]

    @pl.when(core == 1)
    def _():
        whole.start()

    @pl.when(core == 0)
    def _():
        for copy in direct:
            copy.start()

    for s in range(SCANS):
        for c in range(2):
            pad[s, c, 0:16] = jnp.zeros((16, 8, SIDE), F32)
            pad[s, c, 48:64] = jnp.zeros((16, 8, SIDE), F32)

    for copy in fetch:
        copy.wait()

    @pl.when(core == 1)
    def _():
        direct[0].wait_recv()
        passed[0].start()
        passed[1].start()
        for copy in (*direct[1:], *passed):
            copy.wait_recv()

    @pl.when(core == 0)
    def _():
        whole.wait_recv()

    pl.semaphore_wait(known.at[0], len(near_by))
    tell(known.at[1], z_next)

    lane = lax.broadcasted_iota(jnp.int32, (BLK // 8 + 1, 8, SIDE), 2)
    beyond = jnp.where(t == N_TILE - 1, 0.0, 1.0).astype(F32)

    def forward(s):
        top, col = row_ref[s], col_ref[s]
        base = jnp.minimum(top // 8, 15)
        rest = top - base * 8

        def cut(i, carry):
            at = pl.ds(base + i * (BLK // 8), BLK // 8 + 1)
            for c in range(2):
                block = jnp.where(lane >= col, obj[c, at], border[c, at] * beyond)
                block = pltpu.roll(shifted(block, rest), (SIDE - col) % SIDE, axis=2)
                win[s, c, rows(i * BLK, BLK), :] = block.reshape(BLK, SIDE)
            return carry

        lax.fori_loop(0, SIDE // BLK, cut, 0, unroll=4)

        def mode(m):
            pr, pi = probe_ref[m, 0].reshape(SIDE, SIDE), probe_ref[m, 1].reshape(SIDE, SIDE)
            wr, wi = win[s, 0], win[s, 1]
            psi[m, 0:SIDE, :] = (pr * wr - pi * wi).astype(BF16)
            psi[m, SIDE:, :] = (pr * wi + pi * wr).astype(BF16)
            mid = jnp.dot(lf_ref[...], psi[m], preferred_element_type=F32).astype(BF16)
            half[m, :, 0:SIDE] = mid[0:SIDE]
            half[m, :, SIDE:] = mid[SIDE:]
            out = jnp.dot(half[m], rf_ref[...], preferred_element_type=F32).astype(BF16)
            spec[s, m] = out
            wide = out.astype(F32)
            wide = wide * wide
            wide = wide[:, :SIDE] + wide[:, SIDE:]
            power[s] = wide if m == 0 else power[s] + wide

        for m in range(MODES):
            mode(m)

    n_q = SIDE // NY

    def q_rows(index):
        return rows(index * n_q, n_q)

    sums = []
    for s in range(SCANS):
        forward(s)
        sums.append([])
        for k in (2, 1, 3):
            src = power.at[s, q_rows((y + k) % NY), :]
            sums[s].append(sems.start(src, pw.at[s, k - 1], y_on[k - 1]))
    pl.semaphore_wait(known.at[1], 2)
    tell(known.at[2], z_next)
    gathers = []
    for s in range(SCANS):
        for copy in sums[s]:
            copy.wait_recv()
        q = q_rows(y)
        total = power[s, q, :] + pw[s, 0] + pw[s, 1] + pw[s, 2]
        factor[s, q, :] = amp_ref[s, q, :] / jnp.maximum(jnp.sqrt(total), 0.5) - 1.0
        gathers.append([sems.start(factor.at[s, q, :], factor.at[s, q, :], y_on[k - 1]) for k in (2, 1, 3)])

    def backward(s):
        active = jnp.where(s < cnt_ref[0], 1.0, 0.0).astype(F32)

        def mode(m):
            f = factor[s]
            psi[m, 0:SIDE, :] = (spec[s, m, :, :SIDE].astype(F32) * f).astype(BF16)
            psi[m, SIDE:, :] = (spec[s, m, :, SIDE:].astype(F32) * f).astype(BF16)
            mid = jnp.dot(rf_ref[...], psi[m], preferred_element_type=F32).astype(BF16)
            half[m, :, 0:SIDE] = mid[0:SIDE]
            half[m, :, SIDE:] = mid[SIDE:]
            chi = jnp.dot(half[m], lf_ref[...], preferred_element_type=F32) * active
            cr, ci = chi[:, :SIDE], chi[:, SIDE:]
            pr, pi = probe_ref[m, 0].reshape(SIDE, SIDE), probe_ref[m, 1].reshape(SIDE, SIDE)
            wr, wi = win[s, 0], win[s, 1]
            gr = (pr * cr + pi * ci).reshape(SIDE // 8, 8, SIDE)
            gi = (pr * ci - pi * cr).reshape(SIDE // 8, 8, SIDE)
            pad[s, 0, 16:48] = gr if m == 0 else pad[s, 0, 16:48] + gr
            pad[s, 1, 16:48] = gi if m == 0 else pad[s, 1, 16:48] + gi
            pgr = (wr * cr + wi * ci).reshape(NZ, NX, 8, SIDE)
            pgi = (wr * ci - wi * cr).reshape(NZ, NX, 8, SIDE)
            if s == 0:
                pgrad[m, 0] = pgr
                pgrad[m, 1] = pgi
            else:
                pgrad[m, 0] = pgrad[m, 0] + pgr
                pgrad[m, 1] = pgrad[m, 1] + pgi

        return mode

    def place(s):
        col, down = col_ref[s], 128 - row_ref[s]
        base = jnp.minimum(down // 8, 15)

        def rows_of(i, carry):
            at = rows(i * BLK, BLK)
            for c in range(2):
                block = pad[s, c, pl.ds(base + i * (BLK // 8), BLK // 8 + 1)]
                block = pltpu.roll(shifted(block, down - base * 8), col, axis=2)
                here = lane[1:] >= col
                inside = jnp.where(here, block, 0.0).reshape(BLK, SIDE)
                outside = jnp.where(here, 0.0, block).reshape(BLK, SIDE)
                own[c, at, :] = inside if s == 0 else own[c, at, :] + inside
                edge[c, at, :] = outside if s == 0 else edge[c, at, :] + outside
            return carry

        lax.fori_loop(0, ROWS // BLK, rows_of, 0, unroll=4)

    core_sum = []
    for s in range(SCANS):
        for copy in gathers[s]:
            copy.wait_recv()
        if s == SCANS - 1:
            pl.semaphore_wait(known.at[2], 2)
        mode = backward(s)
        for m in range(MODES):
            mode(m)
            if s == SCANS - 1:
                core_sum.append(sems.start(pgrad.at[m, 1 - core], p_core.at[m], peer))
        if s < SCANS - 1:
            place(s)

    quarter_rows = ROWS // NY

    def quarter(index):
        return rows(index * quarter_rows, quarter_rows)

    def object_flow():
        yield 0.5
        place(SCANS - 1)

        core_edge = sems.make(edge, from_core, peer)
        far = (2, 1, 3)
        edge_sum = [sems.make(edge.at[:, quarter((y + k) % NY), :], re.at[k - 1], y_on[k - 1]) for k in far]
        n_cross = 4
        n_part = quarter_rows // n_cross
        cross = []
        for c in range(2):
            for i in range(n_cross):
                src = edge.at[c, rows(y * quarter_rows + i * n_part, n_part), :]
                cross.append(sems.make(src, arrive.at[c, rows(i * n_part, n_part), :], t_right))
        own_sum = {}
        for c in range(2):
            for k in far:
                src = own.at[c, quarter((y + k) % NY), :]
                own_sum[c, k] = sems.make(src, ro.at[k - 1, c], y_on[k - 1])
        spread = {}
        for c in range(2):
            here = onew_ref.at[c, quarter(y), :]
            for k in far:
                spread[c, k] = sems.make(here, here, y_on[k - 1])
        q8 = pl.ds(y * (quarter_rows // 8), quarter_rows // 8)
        inner = jnp.where(t == 0, 0.0, 1.0).astype(F32)

        def finish(c, on_core):
            @pl.when(core == on_core)
            def _():
                if on_core == 0:
                    for copy in cross[c * n_cross : (c + 1) * n_cross]:
                        copy.wait_recv()
                for k in far:
                    own_sum[c, k].wait_recv()
                total = own[c, quarter(y), :] + ro[0, c] + ro[1, c] + ro[2, c]
                if on_core == 0:
                    total = total + arrive[c] * inner
                onew_ref[c, quarter(y), :] = obj[c, q8].reshape(quarter_rows, SIDE) + total
                for k in far:
                    spread[c, k].start()

        @pl.when(core == 0)
        def _():
            core_edge.start()

        @pl.when(core == 1)
        def _():
            for copy in edge_sum:
                copy.start()

        yield 4.5

        @pl.when(core == 0)
        def _():
            core_edge.wait_send()

        @pl.when(core == 1)
        def _():
            core_edge.wait_recv()
            own[...] = own[...] + from_core[...]

        for copy in own_sum.values():
            copy.start()
        yield 10.0

        @pl.when(core == 1)
        def _():
            for copy in edge_sum:
                copy.wait_recv()
            edge[:, quarter(y), :] = edge[:, quarter(y), :] + re[0] + re[1] + re[2]
            cross[0].start()

        for i in range(1, 2 * n_cross):
            yield 10.0 + 0.7 * i
            if i == 4:
                finish(0, 1)

            @pl.when(core == 1)
            def _(copy=cross[i]):
                copy.start()

        yield 15.6
        finish(0, 0)
        yield 16.4
        finish(1, 1)
        yield 18.2
        finish(1, 0)
        yield 27.0
        for copy in spread.values():
            copy.wait_recv()
        sems.started += [*own_sum.values(), *spread.values()]

        @pl.when(core == 1)
        def _():
            for copy in (*edge_sum, *cross):
                copy.wait_send()

    def probe_flow(m):
        begin = 0.2 + 2.8 * m
        grad, new = pgrad.at[m, core], pnew_ref.at[m, core]
        yield 0.2 + 0.8 * m
        core_sum[m].wait_recv()
        grad[...] = grad[...] + p_core[m]
        x_sum, z_sum = {}, {}
        for k in Z_ORDER:
            for d in (2, 1, 3):
                src = grad.at[(z + k) % NZ, (x + d) % NX]
                x_sum[k, d] = sems.start(src, px.at[m, k, d - 1], x_on[d - 1])
        for j, k in enumerate(Z_ORDER):
            yield begin + 3.7 + 0.35 * j
            for d in (2, 1, 3):
                x_sum[k, d].wait_recv()
            zz = (z + k) % NZ
            grad[zz, x] = grad[zz, x] + px[m, k, 0] + px[m, k, 1] + px[m, k, 2]
            if k:
                z_sum[k] = sems.start(grad.at[zz, x], pz.at[m, k - 1], z_dev[k - 1])
        yield begin + 9.0
        total = grad[z, x]
        for k in Z_ORDER[:-1]:
            z_sum[k].wait_recv()
            total = total + pz[m, k - 1]
        new[z, x] = probe_ref[m, core, z, x] + total * 0.5

        def share(at, dev):
            return sems.start(new.at[at], new.at[at], dev)

        core_all = []
        z_all = {k: share((z, x), z_dev[k - 1]) for k in Z_ORDER[:-1]}
        x_all = {}
        for j, k in enumerate(Z_ORDER[::-1]):
            if k:
                yield begin + 11.8 + 0.3 * j
                z_all[k].wait_recv()
            for d in (2, 1, 3):
                x_all[k, d] = share(((z + NZ - k) % NZ, x), x_on[d - 1])
        for j, k in enumerate(Z_ORDER[::-1]):
            yield begin + 15.8 + 0.3 * j
            for d in (1, 3, 2):
                x_all[k, d].wait_recv()
            core_all.append(share(((z + NZ - k) % NZ,), peer))
        yield begin + 19.5
        for copy in core_all:
            copy.wait_recv()

    flows = [object_flow(), *(probe_flow(m) for m in range(MODES))]
    due = [next(flow) for flow in flows]
    while flows:
        i = due.index(min(due))
        at = next(flows[i], None)
        if at is None:
            del flows[i], due[i]
        else:
            due[i] = at

    for copy in sems.started:
        copy.wait_send()

    @pl.when(core == 1)
    def _():
        for copy in (whole, *passed):
            copy.wait_send()

    @pl.when(core == 0)
    def _():
        for copy in direct:
            copy.wait_send()


def on_device(object_tile, probe, amplitudes, row_offsets, col_offsets, scan_count):
    left, right = dft_blocks()
    vmem = pl.BlockSpec(memory_space=pltpu.VMEM)
    smem = pl.BlockSpec(memory_space=pltpu.SMEM)
    stacked = (MODES, 2, NZ, NX, 8, SIDE)
    anywhere = pl.BlockSpec(memory_space=pl.ANY)
    scratch = [
        pltpu.VMEM((2, ROWS // 8, 8, SIDE), F32),
        pltpu.VMEM(stacked, F32),
        pltpu.VMEM((SCANS, SIDE, SIDE), F32),
        pltpu.VMEM((2 * SIDE, 2 * SIDE), BF16),
        pltpu.VMEM((2 * SIDE, 2 * SIDE), BF16),
        pltpu.VMEM((2, ROWS // 8, 8, SIDE), F32),
        pltpu.VMEM((SCANS, 2, SIDE, SIDE), F32),
        pltpu.VMEM((MODES, 2 * SIDE, SIDE), BF16),
        pltpu.VMEM((MODES, SIDE, 2 * SIDE), BF16),
        pltpu.VMEM((SCANS, MODES, SIDE, 2 * SIDE), BF16),
        pltpu.VMEM((SCANS, SIDE, SIDE), F32),
        pltpu.VMEM((SCANS, NY - 1, SIDE // NY, SIDE), F32),
        pltpu.VMEM((SCANS, SIDE, SIDE), F32),
        pltpu.VMEM((SCANS, 2, 2 * SIDE // 8, 8, SIDE), F32),
        pltpu.VMEM(stacked, F32),
        pltpu.VMEM((MODES, NZ, NX, 8, SIDE), F32),
        pltpu.VMEM((MODES, NZ, NX - 1, 8, SIDE), F32),
        pltpu.VMEM((MODES, NZ - 1, 8, SIDE), F32),
        pltpu.VMEM((2, ROWS, SIDE), F32),
        pltpu.VMEM((2, ROWS, SIDE), F32),
        pltpu.VMEM((2, ROWS, SIDE), F32),
        pltpu.VMEM((NY - 1, 2, ROWS // NY, SIDE), F32),
        pltpu.VMEM((NY - 1, 2, ROWS // NY, SIDE), F32),
        pltpu.VMEM((2, ROWS // 4, SIDE), F32),
        pltpu.SemaphoreType.DMA((N_SEMS,)),
        pltpu.SemaphoreType.DMA((N_SEMS,)),
        pltpu.SemaphoreType.DMA((5,)),
        pltpu.SemaphoreType.REGULAR((3,)),
    ]
    object_new, probe_new = pl.pallas_call(
        kernel,
        out_shape=(
            pltpu.VMEM(object_tile.shape, F32),
            pltpu.VMEM(stacked, F32),
        ),
        in_specs=[smem] * 3 + [anywhere] * 5,
        out_specs=(vmem, vmem),
        scratch_shapes=scratch,
        compiler_params=pltpu.CompilerParams(
            collective_id=0, has_side_effects=True, vmem_limit_bytes=56 * 1024 * 1024
        ),
        cost_estimate=pl.CostEstimate(flops=3_300_000_000, bytes_accessed=6_000_000, transcendentals=131072),
    )(
        row_offsets,
        col_offsets,
        scan_count,
        object_tile.reshape(2, ROWS // 8, 8, SIDE),
        probe.reshape(stacked),
        amplitudes,
        jnp.asarray(left),
        jnp.asarray(right),
    )
    return object_new, probe_new.reshape(probe.shape)


def solution(mesh):
    in_specs = (
        P(None, None, "tile"),
        P("mode", None, None, None),
        P("tile", None, None),
        P("tile"),
        P("tile"),
        P("tile"),
    )
    out_specs = (P(None, None, "tile"), P("mode", None, None, None))
    return jax.shard_map(on_device, mesh=mesh, in_specs=in_specs, out_specs=out_specs, check_vma=False)
```

```python
import functools

import jax
import jax.numpy as jnp
import numpy as np
from jax import lax
from jax.experimental import pallas as pl
from jax.experimental.pallas import tpu as pltpu
from jax.sharding import PartitionSpec as P

SIDE = 256
ROWS = 384
MODES = 3
SCANS = 2
NX, NZ, NY = 4, 8, 4
N_TILE = 64
F32 = jnp.float32
BF16 = jnp.bfloat16
BLK = 32


def dft_blocks():
    counter = np.arange(SIDE)
    phase = (np.outer(counter, counter) % SIDE) * (2.0 * np.pi / SIDE)
    real = np.cos(phase) / np.sqrt(SIDE)
    imag = -np.sin(phase) / np.sqrt(SIDE)
    left = np.block([[real, -imag], [imag, real]])
    right = np.block([[real, imag], [-imag, real]])
    return left.astype(np.float32).astype(jnp.bfloat16), right.astype(np.float32).astype(jnp.bfloat16)


class Sems:
    def __init__(self, send, recv):
        self.send, self.recv, self.used, self.started = send, recv, 0, []

    def make(self, src, dst, dev):
        i = self.used
        self.used += 1
        copy = pltpu.make_async_remote_copy(
            src_ref=src,
            dst_ref=dst,
            send_sem=self.send.at[i],
            recv_sem=self.recv.at[i],
            device_id=dev,
            device_id_type=pl.DeviceIdType.MESH,
        )
        return copy

    def start(self, src, dst, dev):
        copy = self.make(src, dst, dev)
        copy.start()
        self.started.append(copy)
        return copy


N_SEMS = 288
Z_ORDER = (4, 3, 5, 2, 6, 1, 7, 0)


def rows(start, size):
    return pl.ds(pl.multiple_of(start, 8), size)


def shifted(blocks, rest):
    turned = pltpu.roll(blocks, (16 - rest) % 8, axis=1)
    row = lax.broadcasted_iota(jnp.int32, turned[1:].shape, 1)
    return jnp.where(row < 8 - rest, turned[:-1], turned[1:])


def kernel(
    row_ref, col_ref, cnt_ref, obj_hbm, probe_hbm, amp_hbm, lf_hbm, rf_hbm,
    onew_ref, pnew_ref,
    obj, probe_ref, amp_ref, lf_ref, rf_ref,
    border, win, psi, half, spec, power, pw, factor, pad, pgrad, p_core,
    px, pz, own, edge, from_core, ro, re, arrive,
    send_sem, recv_sem, fetch_sem, known,
):
    t = lax.axis_index("tile")
    y = lax.axis_index("mode")
    core = t % 2
    z = (t // 2) % NZ
    x = t // (2 * NZ)
    sems = Sems(send_sem, recv_sem)

    def tile_dev(xx, zz, cc):
        return ((xx * NZ + zz) * 2 + cc, y)

    t_left = ((t + N_TILE - 1) % N_TILE, y)
    t_right = ((t + 1) % N_TILE, y)
    peer = tile_dev(x, z, 1 - core)

    y_on = [(t, (y + k) % NY) for k in range(1, NY)]
    x_on = [tile_dev((x + k) % NX, z, core) for k in range(1, NX)]
    z_dev = [tile_dev(x, (z + k) % NZ, core) for k in range(1, NZ)]

    fetch = []
    for src, dst in ((obj_hbm, obj), (probe_hbm, probe_ref), (lf_hbm, lf_ref), (rf_hbm, rf_ref), (amp_hbm, amp_ref)):
        fetch.append(pltpu.make_async_copy(src, dst, fetch_sem.at[len(fetch)]))
        fetch[-1].start()

    def tell(semaphore, devices):
        for dev in devices:
            pl.semaphore_signal(semaphore, inc=1, device_id=dev, device_id_type=pl.DeviceIdType.MESH)

    barrier = pltpu.get_barrier_semaphore()
    z_next = [z_dev[0], z_dev[-1]]
    near_by = [y_on[0], y_on[2], x_on[0], x_on[2], *z_next]
    tell(barrier, [t_left, t_right, *near_by])
    pl.semaphore_wait(barrier, 2 + len(near_by))
    tell(known.at[0], near_by)

    def blocks(index, first, last):
        return pl.ds(index * (ROWS // 32) + first, last - first)

    def near(ref, at):
        return ref.at[:, at]

    y_up, y_across, y_down = [(y + k) % NY for k in range(1, NY)]
    whole = sems.make(obj_hbm, border, peer)
    relayed = [blocks(y, 3 * i, 3 * i + 3) for i in range(3)]
    ranges = (*relayed, blocks(y_across, 0, 12), *(blocks(i, 9, 12) for i in (y, y_up, y_down)))
    direct = [sems.make(near(obj_hbm, at), near(border, at), t_left) for at in ranges]
    passed = [sems.make(near(border, at), near(border, at), dev) for at in relayed for dev in (y_on[0], y_on[2])]

    @pl.when(core == 1)
    def _():
        whole.start()

    @pl.when(core == 0)
    def _():
        for copy in direct:
            copy.start()

    for s in range(SCANS):
        for c in range(2):
            pad[s, c, 0:16] = jnp.zeros((16, 8, SIDE), F32)
            pad[s, c, 48:64] = jnp.zeros((16, 8, SIDE), F32)

    for copy in fetch:
        copy.wait()

    @pl.when(core == 1)
    def _():
        for i in range(3):
            direct[i].wait_recv()
            passed[2 * i].start()
            passed[2 * i + 1].start()
        for copy in (*direct[3:], *passed):
            copy.wait_recv()

    @pl.when(core == 0)
    def _():
        whole.wait_recv()

    pl.semaphore_wait(known.at[0], len(near_by))
    tell(known.at[1], z_next)

    lane = lax.broadcasted_iota(jnp.int32, (BLK // 8 + 1, 8, SIDE), 2)
    beyond = jnp.where(t == N_TILE - 1, 0.0, 1.0).astype(F32)

    def forward(s):
        top, col = row_ref[s], col_ref[s]
        base = jnp.minimum(top // 8, 15)
        rest = top - base * 8

        def cut(i, carry):
            at = pl.ds(base + i * (BLK // 8), BLK // 8 + 1)
            for c in range(2):
                block = jnp.where(lane >= col, obj[c, at], border[c, at] * beyond)
                block = pltpu.roll(shifted(block, rest), (SIDE - col) % SIDE, axis=2)
                win[s, c, rows(i * BLK, BLK), :] = block.reshape(BLK, SIDE)
            return carry

        lax.fori_loop(0, SIDE // BLK, cut, 0, unroll=4)

        def mode(m):
            pr, pi = probe_ref[m, 0].reshape(SIDE, SIDE), probe_ref[m, 1].reshape(SIDE, SIDE)
            wr, wi = win[s, 0], win[s, 1]
            psi[m, 0:SIDE, :] = (pr * wr - pi * wi).astype(BF16)
            psi[m, SIDE:, :] = (pr * wi + pi * wr).astype(BF16)
            mid = jnp.dot(lf_ref[...], psi[m], preferred_element_type=F32).astype(BF16)
            half[m, :, 0:SIDE] = mid[0:SIDE]
            half[m, :, SIDE:] = mid[SIDE:]
            out = jnp.dot(half[m], rf_ref[...], preferred_element_type=F32).astype(BF16)
            spec[s, m] = out
            wide = out.astype(F32)
            wide = wide * wide
            wide = wide[:, :SIDE] + wide[:, SIDE:]
            power[s] = wide if m == 0 else power[s] + wide

        for m in range(MODES):
            mode(m)

    n_q = SIDE // NY

    def q_rows(index):
        return rows(index * n_q, n_q)

    sums = []
    for s in range(SCANS):
        forward(s)
        sums.append([])
        for k in (2, 1, 3):
            src = power.at[s, q_rows((y + k) % NY), :]
            sums[s].append(sems.start(src, pw.at[s, k - 1], y_on[k - 1]))
    gathers = []
    for s in range(SCANS):
        for copy in sums[s]:
            copy.wait_recv()
        q = q_rows(y)
        total = power[s, q, :] + pw[s, 0] + pw[s, 1] + pw[s, 2]
        factor[s, q, :] = amp_ref[s, q, :] / jnp.maximum(jnp.sqrt(total), 0.5) - 1.0
        gathers.append([sems.start(factor.at[s, q, :], factor.at[s, q, :], y_on[k - 1]) for k in (2, 1, 3)])
    pl.semaphore_wait(known.at[1], 2)
    tell(known.at[2], z_next)

    def backward(s):
        active = jnp.where(s < cnt_ref[0], 1.0, 0.0).astype(F32)

        def mode(m):
            f = factor[s]
            psi[m, 0:SIDE, :] = (spec[s, m, :, :SIDE].astype(F32) * f).astype(BF16)
            psi[m, SIDE:, :] = (spec[s, m, :, SIDE:].astype(F32) * f).astype(BF16)
            mid = jnp.dot(rf_ref[...], psi[m], preferred_element_type=F32).astype(BF16)
            half[m, :, 0:SIDE] = mid[0:SIDE]
            half[m, :, SIDE:] = mid[SIDE:]
            chi = jnp.dot(half[m], lf_ref[...], preferred_element_type=F32) * active
            cr, ci = chi[:, :SIDE], chi[:, SIDE:]
            pr, pi = probe_ref[m, 0].reshape(SIDE, SIDE), probe_ref[m, 1].reshape(SIDE, SIDE)
            wr, wi = win[s, 0], win[s, 1]
            gr = (pr * cr + pi * ci).reshape(SIDE // 8, 8, SIDE)
            gi = (pr * ci - pi * cr).reshape(SIDE // 8, 8, SIDE)
            pad[s, 0, 16:48] = gr if m == 0 else pad[s, 0, 16:48] + gr
            pad[s, 1, 16:48] = gi if m == 0 else pad[s, 1, 16:48] + gi
            pgr = (wr * cr + wi * ci).reshape(NZ, NX, 8, SIDE)
            pgi = (wr * ci - wi * cr).reshape(NZ, NX, 8, SIDE)
            if s == 0:
                pgrad[m, 0] = pgr
                pgrad[m, 1] = pgi
            else:
                pgrad[m, 0] = pgrad[m, 0] + pgr
                pgrad[m, 1] = pgrad[m, 1] + pgi

        return mode

    def place(s):
        col, down = col_ref[s], 128 - row_ref[s]
        base = jnp.minimum(down // 8, 15)

        def rows_of(i, carry):
            at = rows(i * BLK, BLK)
            for c in range(2):
                block = pad[s, c, pl.ds(base + i * (BLK // 8), BLK // 8 + 1)]
                block = pltpu.roll(shifted(block, down - base * 8), col, axis=2)
                here = lane[1:] >= col
                inside = jnp.where(here, block, 0.0).reshape(BLK, SIDE)
                outside = jnp.where(here, 0.0, block).reshape(BLK, SIDE)
                own[c, at, :] = inside if s == 0 else own[c, at, :] + inside
                edge[c, at, :] = outside if s == 0 else edge[c, at, :] + outside
            return carry

        lax.fori_loop(0, ROWS // BLK, rows_of, 0, unroll=4)

    core_sum = []
    for s in range(SCANS):
        for copy in gathers[s]:
            copy.wait_recv()
        mode = backward(s)
        for m in range(MODES):
            mode(m)
            if s == SCANS - 1:
                core_sum.append(sems.start(pgrad.at[m, 1 - core], p_core.at[m], peer))
        if s < SCANS - 1:
            place(s)

    quarter_rows = ROWS // NY

    def quarter(index):
        return rows(index * quarter_rows, quarter_rows)

    def object_flow():
        yield 0.5
        place(SCANS - 1)

        core_edge = sems.make(edge, from_core, peer)
        far = (2, 1, 3)
        edge_sum = [sems.make(edge.at[:, quarter((y + k) % NY), :], re.at[k - 1], y_on[k - 1]) for k in far]
        n_cross = 4
        n_part = quarter_rows // n_cross
        cross = []
        for c in range(2):
            for i in range(n_cross):
                src = edge.at[c, rows(y * quarter_rows + i * n_part, n_part), :]
                cross.append(sems.make(src, arrive.at[c, rows(i * n_part, n_part), :], t_right))
        own_sum = {}
        for c in range(2):
            for k in far:
                src = own.at[c, quarter((y + k) % NY), :]
                own_sum[c, k] = sems.make(src, ro.at[k - 1, c], y_on[k - 1])
        spread = {}
        for c in range(2):
            here = onew_ref.at[c, quarter(y), :]
            for k in far:
                spread[c, k] = sems.make(here, here, y_on[k - 1])
        q8 = pl.ds(y * (quarter_rows // 8), quarter_rows // 8)
        inner = jnp.where(t == 0, 0.0, 1.0).astype(F32)

        def finish(c, on_core):
            @pl.when(core == on_core)
            def _():
                if on_core == 0:
                    for copy in cross[c * n_cross : (c + 1) * n_cross]:
                        copy.wait_recv()
                for k in far:
                    own_sum[c, k].wait_recv()
                total = own[c, quarter(y), :] + ro[0, c] + ro[1, c] + ro[2, c]
                if on_core == 0:
                    total = total + arrive[c] * inner
                onew_ref[c, quarter(y), :] = obj[c, q8].reshape(quarter_rows, SIDE) + total
                for k in far:
                    spread[c, k].start()

        @pl.when(core == 0)
        def _():
            core_edge.start()

        @pl.when(core == 1)
        def _():
            for copy in edge_sum:
                copy.start()

        yield 4.5

        @pl.when(core == 0)
        def _():
            core_edge.wait_send()

        @pl.when(core == 1)
        def _():
            core_edge.wait_recv()
            own[...] = own[...] + from_core[...]

        for copy in own_sum.values():
            copy.start()
        yield 10.0

        @pl.when(core == 1)
        def _():
            for copy in edge_sum:
                copy.wait_recv()
            edge[:, quarter(y), :] = edge[:, quarter(y), :] + re[0] + re[1] + re[2]
            cross[0].start()

        for i in range(1, 2 * n_cross):
            yield 10.0 + 0.7 * i
            if i == 4:
                finish(0, 1)

            @pl.when(core == 1)
            def _(copy=cross[i]):
                copy.start()

        yield 15.6
        finish(0, 0)
        yield 16.4
        finish(1, 1)
        yield 18.2
        finish(1, 0)
        yield 27.0
        for copy in spread.values():
            copy.wait_recv()
        sems.started += [*own_sum.values(), *spread.values()]

        @pl.when(core == 1)
        def _():
            for copy in (*edge_sum, *cross):
                copy.wait_send()

    def probe_flow(m):
        begin = 0.2 + 2.8 * m
        grad, new = pgrad.at[m, core], pnew_ref.at[m, core]
        yield 0.2 + 0.8 * m
        core_sum[m].wait_recv()
        grad[...] = grad[...] + p_core[m]
        x_sum, z_sum = {}, {}
        for k in Z_ORDER:
            for d in (2, 1, 3):
                src = grad.at[(z + k) % NZ, (x + d) % NX]
                x_sum[k, d] = sems.start(src, px.at[m, k, d - 1], x_on[d - 1])
        for j, k in enumerate(Z_ORDER):
            yield begin + 3.7 + 0.35 * j
            for d in (2, 1, 3):
                x_sum[k, d].wait_recv()
            zz = (z + k) % NZ
            grad[zz, x] = grad[zz, x] + px[m, k, 0] + px[m, k, 1] + px[m, k, 2]
            if k:
                z_sum[k] = sems.start(grad.at[zz, x], pz.at[m, k - 1], z_dev[k - 1])
        yield begin + 9.0
        total = grad[z, x]
        for k in Z_ORDER[:-1]:
            z_sum[k].wait_recv()
            total = total + pz[m, k - 1]
        new[z, x] = probe_ref[m, core, z, x] + total * 0.5

        def share(at, dev):
            return sems.start(new.at[at], new.at[at], dev)

        core_all = []
        z_all = {k: share((z, x), z_dev[k - 1]) for k in Z_ORDER[:-1]}
        x_all = {}
        for j, k in enumerate(Z_ORDER[::-1]):
            if k:
                yield begin + 11.8 + 0.3 * j
                z_all[k].wait_recv()
            for d in (2, 1, 3):
                x_all[k, d] = share(((z + NZ - k) % NZ, x), x_on[d - 1])
        for j, k in enumerate(Z_ORDER[::-1]):
            yield begin + 15.8 + 0.3 * j
            for d in (1, 3, 2):
                x_all[k, d].wait_recv()
            core_all.append(share(((z + NZ - k) % NZ,), peer))
        yield begin + 19.5
        for copy in core_all:
            copy.wait_recv()

    pl.semaphore_wait(known.at[2], 2)
    flows = [object_flow(), *(probe_flow(m) for m in range(MODES))]
    due = [next(flow) for flow in flows]
    while flows:
        i = due.index(min(due))
        at = next(flows[i], None)
        if at is None:
            del flows[i], due[i]
        else:
            due[i] = at

    for copy in sems.started:
        copy.wait_send()

    @pl.when(core == 1)
    def _():
        for copy in (whole, *passed):
            copy.wait_send()

    @pl.when(core == 0)
    def _():
        for copy in direct:
            copy.wait_send()


def on_device(object_tile, probe, amplitudes, row_offsets, col_offsets, scan_count):
    left, right = dft_blocks()
    vmem = pl.BlockSpec(memory_space=pltpu.VMEM)
    smem = pl.BlockSpec(memory_space=pltpu.SMEM)
    stacked = (MODES, 2, NZ, NX, 8, SIDE)
    anywhere = pl.BlockSpec(memory_space=pl.ANY)
    scratch = [
        pltpu.VMEM((2, ROWS // 8, 8, SIDE), F32),
        pltpu.VMEM(stacked, F32),
        pltpu.VMEM((SCANS, SIDE, SIDE), F32),
        pltpu.VMEM((2 * SIDE, 2 * SIDE), BF16),
        pltpu.VMEM((2 * SIDE, 2 * SIDE), BF16),
        pltpu.VMEM((2, ROWS // 8, 8, SIDE), F32),
        pltpu.VMEM((SCANS, 2, SIDE, SIDE), F32),
        pltpu.VMEM((MODES, 2 * SIDE, SIDE), BF16),
        pltpu.VMEM((MODES, SIDE, 2 * SIDE), BF16),
        pltpu.VMEM((SCANS, MODES, SIDE, 2 * SIDE), BF16),
        pltpu.VMEM((SCANS, SIDE, SIDE), F32),
        pltpu.VMEM((SCANS, NY - 1, SIDE // NY, SIDE), F32),
        pltpu.VMEM((SCANS, SIDE, SIDE), F32),
        pltpu.VMEM((SCANS, 2, 2 * SIDE // 8, 8, SIDE), F32),
        pltpu.VMEM(stacked, F32),
        pltpu.VMEM((MODES, NZ, NX, 8, SIDE), F32),
        pltpu.VMEM((MODES, NZ, NX - 1, 8, SIDE), F32),
        pltpu.VMEM((MODES, NZ - 1, 8, SIDE), F32),
        pltpu.VMEM((2, ROWS, SIDE), F32),
        pltpu.VMEM((2, ROWS, SIDE), F32),
        pltpu.VMEM((2, ROWS, SIDE), F32),
        pltpu.VMEM((NY - 1, 2, ROWS // NY, SIDE), F32),
        pltpu.VMEM((NY - 1, 2, ROWS // NY, SIDE), F32),
        pltpu.VMEM((2, ROWS // 4, SIDE), F32),
        pltpu.SemaphoreType.DMA((N_SEMS,)),
        pltpu.SemaphoreType.DMA((N_SEMS,)),
        pltpu.SemaphoreType.DMA((5,)),
        pltpu.SemaphoreType.REGULAR((3,)),
    ]
    object_new, probe_new = pl.pallas_call(
        kernel,
        out_shape=(
            pltpu.VMEM(object_tile.shape, F32),
            pltpu.VMEM(stacked, F32),
        ),
        in_specs=[smem] * 3 + [anywhere] * 5,
        out_specs=(vmem, vmem),
        scratch_shapes=scratch,
        compiler_params=pltpu.CompilerParams(
            collective_id=0, has_side_effects=True, vmem_limit_bytes=56 * 1024 * 1024
        ),
        cost_estimate=pl.CostEstimate(flops=3_300_000_000, bytes_accessed=6_000_000, transcendentals=131072),
    )(
        row_offsets,
        col_offsets,
        scan_count,
        object_tile.reshape(2, ROWS // 8, 8, SIDE),
        probe.reshape(stacked),
        amplitudes,
        jnp.asarray(left),
        jnp.asarray(right),
    )

    def leave(a, b, a_out, b_out, sem):
        copies = [pltpu.make_async_copy(src, dst, sem.at[i]) for i, (src, dst) in enumerate(((a, a_out), (b, b_out)))]
        for copy in copies:
            copy.start()
        for copy in copies:
            copy.wait()

    object_new, probe_new = pl.pallas_call(
        leave,
        out_shape=(jax.ShapeDtypeStruct(object_tile.shape, F32), jax.ShapeDtypeStruct(stacked, F32)),
        in_specs=[anywhere] * 2,
        out_specs=(anywhere, anywhere),
        scratch_shapes=[pltpu.SemaphoreType.DMA((2,))],
        compiler_params=pltpu.CompilerParams(vmem_limit_bytes=16 * 1024 * 1024),
    )(object_new, probe_new)
    return object_new, probe_new.reshape(probe.shape)


def solution(mesh):
    in_specs = (
        P(None, None, "tile"),
        P("mode", None, None, None),
        P("tile", None, None),
        P("tile"),
        P("tile"),
        P("tile"),
    )
    out_specs = (P(None, None, "tile"), P("mode", None, None, None))
    return jax.shard_map(on_device, mesh=mesh, in_specs=in_specs, out_specs=out_specs, check_vma=False)
```

```python
import functools

import jax
import jax.numpy as jnp
import numpy as np
from jax import lax
from jax.experimental import pallas as pl
from jax.experimental.pallas import tpu as pltpu
from jax.sharding import PartitionSpec as P

SIDE = 256
ROWS = 384
MODES = 3
SCANS = 2
NX, NZ, NY = 4, 8, 4
N_TILE = 64
F32 = jnp.float32
BF16 = jnp.bfloat16
BLK = 32


def dft_blocks():
    counter = np.arange(SIDE)
    phase = (np.outer(counter, counter) % SIDE) * (2.0 * np.pi / SIDE)
    real = np.cos(phase) / np.sqrt(SIDE)
    imag = -np.sin(phase) / np.sqrt(SIDE)
    left = np.block([[real, -imag], [imag, real]])
    right = np.block([[real, imag], [-imag, real]])
    return left.astype(np.float32).astype(jnp.bfloat16), right.astype(np.float32).astype(jnp.bfloat16)


class Sems:
    def __init__(self, send, recv):
        self.send, self.recv, self.used, self.started, self.now = send, recv, 0, [], -5.0

    def make(self, src, dst, dev):
        i = self.used
        self.used += 1
        copy = pltpu.make_async_remote_copy(
            src_ref=src,
            dst_ref=dst,
            send_sem=self.send.at[i],
            recv_sem=self.recv.at[i],
            device_id=dev,
            device_id_type=pl.DeviceIdType.MESH,
        )
        return copy

    def start(self, src, dst, dev):
        copy = self.make(src, dst, dev)
        copy.start()
        self.started.append((copy, self.now))
        return copy

    def settle(self, now):
        old = [copy for copy, at in self.started if at + 8.0 < now]
        self.started = [(copy, at) for copy, at in self.started if at + 8.0 >= now]
        for copy in old:
            copy.wait_send()


N_SEMS = 288
Z_ORDER = (4, 3, 5, 2, 6, 1, 7, 0)


def rows(start, size):
    return pl.ds(pl.multiple_of(start, 8), size)


def shifted(blocks, rest):
    turned = pltpu.roll(blocks, (16 - rest) % 8, axis=1)
    row = lax.broadcasted_iota(jnp.int32, turned[1:].shape, 1)
    return jnp.where(row < 8 - rest, turned[:-1], turned[1:])


def kernel(
    row_ref, col_ref, cnt_ref, obj_hbm, probe_hbm, amp_hbm, lf_hbm, rf_hbm,
    onew_ref, pnew_ref,
    obj, probe_ref, amp_ref, lf_ref, rf_ref,
    border, win, psi, half, spec, power, pw, factor, pad, pgrad, p_core,
    px, pz, own, edge, from_core, ro, re, arrive,
    send_sem, recv_sem, fetch_sem, known,
):
    t = lax.axis_index("tile")
    y = lax.axis_index("mode")
    core = t % 2
    z = (t // 2) % NZ
    x = t // (2 * NZ)
    sems = Sems(send_sem, recv_sem)

    def tile_dev(xx, zz, cc):
        return ((xx * NZ + zz) * 2 + cc, y)

    t_left = ((t + N_TILE - 1) % N_TILE, y)
    t_right = ((t + 1) % N_TILE, y)
    peer = tile_dev(x, z, 1 - core)

    y_on = [(t, (y + k) % NY) for k in range(1, NY)]
    x_on = [tile_dev((x + k) % NX, z, core) for k in range(1, NX)]
    z_dev = [tile_dev(x, (z + k) % NZ, core) for k in range(1, NZ)]

    def tell(semaphore, devices):
        for dev in devices:
            pl.semaphore_signal(semaphore, inc=1, device_id=dev, device_id_type=pl.DeviceIdType.MESH)

    barrier = pltpu.get_barrier_semaphore()
    z_next = [z_dev[0], z_dev[-1]]
    near_by = [y_on[0], y_on[2], x_on[0], x_on[2], *z_next]
    tell(barrier, [t_left, t_right, *near_by])
    fetch = []
    for src, dst in ((obj_hbm, obj), (probe_hbm, probe_ref), (lf_hbm, lf_ref), (rf_hbm, rf_ref), (amp_hbm, amp_ref)):
        fetch.append(pltpu.make_async_copy(src, dst, fetch_sem.at[len(fetch)]))
        fetch[-1].start()
    pl.semaphore_wait(barrier, 2 + len(near_by))
    tell(known.at[0], near_by)

    def blocks(index, first, last):
        return pl.ds(index * (ROWS // 32) + first, last - first)

    def near(ref, at):
        return ref.at[:, at]

    y_up, y_across, y_down = [(y + k) % NY for k in range(1, NY)]
    whole = sems.make(obj_hbm, border, peer)
    relayed = [blocks(y, 3 * i, 3 * i + 3) for i in range(3)]
    ranges = (*relayed, blocks(y_across, 0, 12), *(blocks(i, 9, 12) for i in (y, y_up, y_down)))
    direct = [sems.make(near(obj_hbm, at), near(border, at), t_left) for at in ranges]
    passed = [sems.make(near(border, at), near(border, at), dev) for at in relayed for dev in (y_on[0], y_on[2])]

    @pl.when(core == 1)
    def _():
        whole.start()

    @pl.when(core == 0)
    def _():
        for copy in direct:
            copy.start()

    for s in range(SCANS):
        for c in range(2):
            pad[s, c, 0:16] = jnp.zeros((16, 8, SIDE), F32)
            pad[s, c, 48:64] = jnp.zeros((16, 8, SIDE), F32)

    for copy in fetch:
        copy.wait()

    @pl.when(core == 1)
    def _():
        for i in range(3):
            direct[i].wait_recv()
            passed[2 * i].start()
            passed[2 * i + 1].start()
        for copy in (*direct[3:], *passed):
            copy.wait_recv()

    @pl.when(core == 0)
    def _():
        whole.wait_recv()

    pl.semaphore_wait(known.at[0], len(near_by))
    tell(known.at[1], z_next)

    lane = lax.broadcasted_iota(jnp.int32, (BLK // 8 + 1, 8, SIDE), 2)
    beyond = jnp.where(t == N_TILE - 1, 0.0, 1.0).astype(F32)

    def forward(s):
        top, col = row_ref[s], col_ref[s]
        base = jnp.minimum(top // 8, 15)
        rest = top - base * 8

        def cut(i, carry):
            at = pl.ds(base + i * (BLK // 8), BLK // 8 + 1)
            for c in range(2):
                block = jnp.where(lane >= col, obj[c, at], border[c, at] * beyond)
                block = pltpu.roll(shifted(block, rest), (SIDE - col) % SIDE, axis=2)
                win[s, c, rows(i * BLK, BLK), :] = block.reshape(BLK, SIDE)
            return carry

        lax.fori_loop(0, SIDE // BLK, cut, 0, unroll=8)

        def mode(m):
            pr, pi = probe_ref[m, 0].reshape(SIDE, SIDE), probe_ref[m, 1].reshape(SIDE, SIDE)
            wr, wi = win[s, 0], win[s, 1]
            psi[m, 0:SIDE, :] = (pr * wr - pi * wi).astype(BF16)
            psi[m, SIDE:, :] = (pr * wi + pi * wr).astype(BF16)
            mid = jnp.dot(lf_ref[...], psi[m], preferred_element_type=F32).astype(BF16)
            half[m, :, 0:SIDE] = mid[0:SIDE]
            half[m, :, SIDE:] = mid[SIDE:]
            out = jnp.dot(half[m], rf_ref[...], preferred_element_type=F32).astype(BF16)
            spec[s, m] = out
            wide = out.astype(F32)
            wide = wide * wide
            wide = wide[:, :SIDE] + wide[:, SIDE:]
            power[s] = wide if m == 0 else power[s] + wide

        for m in range(MODES):
            mode(m)

    n_q = SIDE // NY

    def q_rows(index):
        return rows(index * n_q, n_q)

    sums = []
    for s in range(SCANS):
        forward(s)
        sums.append([])
        for k in (2, 1, 3):
            src = power.at[s, q_rows((y + k) % NY), :]
            sums[s].append(sems.start(src, pw.at[s, k - 1], y_on[k - 1]))
    gathers = []
    for s in range(SCANS):
        for copy in sums[s]:
            copy.wait_recv()
        active = jnp.where(s < cnt_ref[0], 1.0, 0.0).astype(F32)
        q = q_rows(y)
        total = power[s, q, :] + pw[s, 0] + pw[s, 1] + pw[s, 2]
        factor[s, q, :] = amp_ref[s, q, :] / jnp.maximum(jnp.sqrt(total), 0.5) - 1.0
        factor[s, q, :] = factor[s, q, :] * active
        gathers.append([sems.start(factor.at[s, q, :], factor.at[s, q, :], y_on[k - 1]) for k in (2, 1, 3)])
    pl.semaphore_wait(known.at[1], 2)
    tell(known.at[2], z_next)

    def backward(s):
        def mode(m):
            f = factor[s]
            psi[m, 0:SIDE, :] = (spec[s, m, :, :SIDE].astype(F32) * f).astype(BF16)
            psi[m, SIDE:, :] = (spec[s, m, :, SIDE:].astype(F32) * f).astype(BF16)
            mid = jnp.dot(rf_ref[...], psi[m], preferred_element_type=F32).astype(BF16)
            half[m, :, 0:SIDE] = mid[0:SIDE]
            half[m, :, SIDE:] = mid[SIDE:]
            chi = jnp.dot(half[m], lf_ref[...], preferred_element_type=F32)
            cr, ci = chi[:, :SIDE], chi[:, SIDE:]
            pr, pi = probe_ref[m, 0].reshape(SIDE, SIDE), probe_ref[m, 1].reshape(SIDE, SIDE)
            wr, wi = win[s, 0], win[s, 1]
            gr = (pr * cr + pi * ci).reshape(SIDE // 8, 8, SIDE)
            gi = (pr * ci - pi * cr).reshape(SIDE // 8, 8, SIDE)
            pad[s, 0, 16:48] = gr if m == 0 else pad[s, 0, 16:48] + gr
            pad[s, 1, 16:48] = gi if m == 0 else pad[s, 1, 16:48] + gi
            pgr = (wr * cr + wi * ci).reshape(NZ, NX, 8, SIDE)
            pgi = (wr * ci - wi * cr).reshape(NZ, NX, 8, SIDE)
            if s == 0:
                pgrad[m, 0] = pgr
                pgrad[m, 1] = pgi
            else:
                pgrad[m, 0] = pgrad[m, 0] + pgr
                pgrad[m, 1] = pgrad[m, 1] + pgi

        return mode

    def place(s):
        col, down = col_ref[s], 128 - row_ref[s]
        base = jnp.minimum(down // 8, 15)

        def rows_of(i, carry):
            at = rows(i * BLK, BLK)
            for c in range(2):
                block = pad[s, c, pl.ds(base + i * (BLK // 8), BLK // 8 + 1)]
                block = pltpu.roll(shifted(block, down - base * 8), col, axis=2)
                here = lane[1:] >= col
                inside = jnp.where(here, block, 0.0).reshape(BLK, SIDE)
                outside = jnp.where(here, 0.0, block).reshape(BLK, SIDE)
                own[c, at, :] = inside if s == 0 else own[c, at, :] + inside
                edge[c, at, :] = outside if s == 0 else edge[c, at, :] + outside
            return carry

        lax.fori_loop(0, ROWS // BLK, rows_of, 0, unroll=4)

    core_sum = []
    for s in range(SCANS):
        for copy in gathers[s]:
            copy.wait_recv()
        mode = backward(s)
        for m in range(MODES):
            mode(m)
            if s == SCANS - 1:
                core_sum.append(sems.start(pgrad.at[m, 1 - core], p_core.at[m], peer))
        if s < SCANS - 1:
            place(s)

    quarter_rows = ROWS // NY

    def quarter(index):
        return rows(index * quarter_rows, quarter_rows)

    def object_flow():
        yield 0.5
        place(SCANS - 1)

        core_edge = sems.make(edge, from_core, peer)
        far = (2, 1, 3)
        edge_sum = [sems.make(edge.at[:, quarter((y + k) % NY), :], re.at[k - 1], y_on[k - 1]) for k in far]
        n_cross = 4
        n_part = quarter_rows // n_cross
        cross = []
        for c in range(2):
            for i in range(n_cross):
                src = edge.at[c, rows(y * quarter_rows + i * n_part, n_part), :]
                cross.append(sems.make(src, arrive.at[c, rows(i * n_part, n_part), :], t_right))
        own_sum = {}
        for c in range(2):
            for k in far:
                src = own.at[c, quarter((y + k) % NY), :]
                own_sum[c, k] = sems.make(src, ro.at[k - 1, c], y_on[k - 1])
        spread = {}
        for c in range(2):
            here = onew_ref.at[c, quarter(y), :]
            for k in far:
                spread[c, k] = sems.make(here, here, y_on[k - 1])
        q8 = pl.ds(y * (quarter_rows // 8), quarter_rows // 8)
        inner = jnp.where(t == 0, 0.0, 1.0).astype(F32)

        def finish(c, on_core):
            @pl.when(core == on_core)
            def _():
                if on_core == 0:
                    for copy in cross[c * n_cross : (c + 1) * n_cross]:
                        copy.wait_recv()
                for k in far:
                    own_sum[c, k].wait_recv()
                total = own[c, quarter(y), :] + ro[0, c] + ro[1, c] + ro[2, c]
                if on_core == 0:
                    total = total + arrive[c] * inner
                onew_ref[c, quarter(y), :] = obj[c, q8].reshape(quarter_rows, SIDE) + total
                for k in far:
                    spread[c, k].start()

        @pl.when(core == 0)
        def _():
            core_edge.start()

        @pl.when(core == 1)
        def _():
            for copy in edge_sum:
                copy.start()

        yield 4.5

        @pl.when(core == 0)
        def _():
            for copy in (*direct, core_edge):
                copy.wait_send()

        @pl.when(core == 1)
        def _():
            for copy in (whole, *passed):
                copy.wait_send()
            core_edge.wait_recv()
            own[...] = own[...] + from_core[...]

        for copy in own_sum.values():
            copy.start()
        sems.started += [(copy, sems.now + 8.0) for copy in own_sum.values()]
        yield 10.0

        @pl.when(core == 1)
        def _():
            for copy in edge_sum:
                copy.wait_recv()
            edge[:, quarter(y), :] = edge[:, quarter(y), :] + re[0] + re[1] + re[2]
            cross[0].start()

        for i in range(1, 2 * n_cross):
            yield 10.0 + 0.35 * i
            if i == 7:
                finish(0, 1)

            @pl.when(core == 1)
            def _(copy=cross[i]):
                copy.start()

        yield 15.6
        finish(0, 0)
        yield 16.4
        finish(1, 1)
        yield 18.2
        finish(1, 0)
        sems.started += [(copy, sems.now) for copy in spread.values()]

        @pl.when(core == 1)
        def _():
            for copy in (*edge_sum, *cross):
                copy.wait_send()

        yield 27.0
        for copy in spread.values():
            copy.wait_recv()

    def probe_flow(m):
        begin = 0.2 + 2.8 * m
        grad, new = pgrad.at[m, core], pnew_ref.at[m, core]
        yield 0.2 + 0.8 * m
        core_sum[m].wait_recv()
        grad[...] = grad[...] + p_core[m]
        x_sum, z_sum = {}, {}
        for k in Z_ORDER:
            for d in (2, 1, 3):
                src = grad.at[(z + k) % NZ, (x + d) % NX]
                x_sum[k, d] = sems.start(src, px.at[m, k, d - 1], x_on[d - 1])
        for j, k in enumerate(Z_ORDER):
            yield begin + 3.7 + 0.35 * j
            for d in (2, 1, 3):
                x_sum[k, d].wait_recv()
            zz = (z + k) % NZ
            grad[zz, x] = grad[zz, x] + px[m, k, 0] + px[m, k, 1] + px[m, k, 2]
            if k:
                z_sum[k] = sems.start(grad.at[zz, x], pz.at[m, k - 1], z_dev[k - 1])
        yield begin + 9.0
        total = grad[z, x]
        for k in Z_ORDER[:-1]:
            z_sum[k].wait_recv()
            total = total + pz[m, k - 1]
        new[z, x] = probe_ref[m, core, z, x] + total * 0.5

        def share(at, dev):
            return sems.start(new.at[at], new.at[at], dev)

        core_all = []
        z_all = {k: share((z, x), z_dev[k - 1]) for k in Z_ORDER[:-1]}
        x_all = {}
        for j, k in enumerate(Z_ORDER[::-1]):
            if k:
                yield begin + 11.8 + 0.3 * j
                z_all[k].wait_recv()
            for d in (2, 1, 3):
                x_all[k, d] = share(((z + NZ - k) % NZ, x), x_on[d - 1])
        for j, k in enumerate(Z_ORDER[::-1]):
            yield begin + 15.8 + 0.3 * j
            for d in (1, 3, 2):
                x_all[k, d].wait_recv()
            core_all.append(share(((z + NZ - k) % NZ,), peer))
        yield begin + 19.5
        for copy in core_all:
            copy.wait_recv()

    pl.semaphore_wait(known.at[2], 2)
    flows = [object_flow(), *(probe_flow(m) for m in range(MODES))]
    sems.now = 0.0
    due = [next(flow) for flow in flows]
    while flows:
        i = due.index(min(due))
        sems.now = due[i]
        sems.settle(sems.now)
        at = next(flows[i], None)
        if at is None:
            del flows[i], due[i]
        else:
            due[i] = at
    sems.settle(1000.0)


def on_device(object_tile, probe, amplitudes, row_offsets, col_offsets, scan_count):
    left, right = dft_blocks()
    vmem = pl.BlockSpec(memory_space=pltpu.VMEM)
    smem = pl.BlockSpec(memory_space=pltpu.SMEM)
    stacked = (MODES, 2, NZ, NX, 8, SIDE)
    anywhere = pl.BlockSpec(memory_space=pl.ANY)
    scratch = [
        pltpu.VMEM((2, ROWS // 8, 8, SIDE), F32),
        pltpu.VMEM(stacked, F32),
        pltpu.VMEM((SCANS, SIDE, SIDE), F32),
        pltpu.VMEM((2 * SIDE, 2 * SIDE), BF16),
        pltpu.VMEM((2 * SIDE, 2 * SIDE), BF16),
        pltpu.VMEM((2, ROWS // 8, 8, SIDE), F32),
        pltpu.VMEM((SCANS, 2, SIDE, SIDE), F32),
        pltpu.VMEM((MODES, 2 * SIDE, SIDE), BF16),
        pltpu.VMEM((MODES, SIDE, 2 * SIDE), BF16),
        pltpu.VMEM((SCANS, MODES, SIDE, 2 * SIDE), BF16),
        pltpu.VMEM((SCANS, SIDE, SIDE), F32),
        pltpu.VMEM((SCANS, NY - 1, SIDE // NY, SIDE), F32),
        pltpu.VMEM((SCANS, SIDE, SIDE), F32),
        pltpu.VMEM((SCANS, 2, 2 * SIDE // 8, 8, SIDE), F32),
        pltpu.VMEM(stacked, F32),
        pltpu.VMEM((MODES, NZ, NX, 8, SIDE), F32),
        pltpu.VMEM((MODES, NZ, NX - 1, 8, SIDE), F32),
        pltpu.VMEM((MODES, NZ - 1, 8, SIDE), F32),
        pltpu.VMEM((2, ROWS, SIDE), F32),
        pltpu.VMEM((2, ROWS, SIDE), F32),
        pltpu.VMEM((2, ROWS, SIDE), F32),
        pltpu.VMEM((NY - 1, 2, ROWS // NY, SIDE), F32),
        pltpu.VMEM((NY - 1, 2, ROWS // NY, SIDE), F32),
        pltpu.VMEM((2, ROWS // 4, SIDE), F32),
        pltpu.SemaphoreType.DMA((N_SEMS,)),
        pltpu.SemaphoreType.DMA((N_SEMS,)),
        pltpu.SemaphoreType.DMA((5,)),
        pltpu.SemaphoreType.REGULAR((3,)),
    ]
    object_new, probe_new = pl.pallas_call(
        kernel,
        out_shape=(
            pltpu.VMEM(object_tile.shape, F32),
            pltpu.VMEM(stacked, F32),
        ),
        in_specs=[smem] * 3 + [anywhere] * 5,
        out_specs=(vmem, vmem),
        scratch_shapes=scratch,
        compiler_params=pltpu.CompilerParams(
            collective_id=0, has_side_effects=True, vmem_limit_bytes=56 * 1024 * 1024
        ),
        cost_estimate=pl.CostEstimate(flops=3_300_000_000, bytes_accessed=6_000_000, transcendentals=131072),
    )(
        row_offsets,
        col_offsets,
        scan_count,
        object_tile.reshape(2, ROWS // 8, 8, SIDE),
        probe.reshape(stacked),
        amplitudes,
        jnp.asarray(left),
        jnp.asarray(right),
    )

    def leave(a, b, a_out, b_out, sem):
        copies = [pltpu.make_async_copy(src, dst, sem.at[i]) for i, (src, dst) in enumerate(((a, a_out), (b, b_out)))]
        for copy in copies:
            copy.start()
        for copy in copies:
            copy.wait()

    object_new, probe_new = pl.pallas_call(
        leave,
        out_shape=(jax.ShapeDtypeStruct(object_tile.shape, F32), jax.ShapeDtypeStruct(stacked, F32)),
        in_specs=[anywhere] * 2,
        out_specs=(anywhere, anywhere),
        scratch_shapes=[pltpu.SemaphoreType.DMA((2,))],
        compiler_params=pltpu.CompilerParams(vmem_limit_bytes=16 * 1024 * 1024),
    )(object_new, probe_new)
    return object_new, probe_new.reshape(probe.shape)


def solution(mesh):
    in_specs = (
        P(None, None, "tile"),
        P("mode", None, None, None),
        P("tile", None, None),
        P("tile"),
        P("tile"),
        P("tile"),
    )
    out_specs = (P(None, None, "tile"), P("mode", None, None, None))
    return jax.shard_map(on_device, mesh=mesh, in_specs=in_specs, out_specs=out_specs, check_vma=False)
```

```python
import functools

import jax
import jax.numpy as jnp
import numpy as np
from jax import lax
from jax.experimental import pallas as pl
from jax.experimental.pallas import tpu as pltpu
from jax.sharding import PartitionSpec as P

SIDE = 256
ROWS = 384
MODES = 3
SCANS = 2
NX, NZ, NY = 4, 8, 4
N_TILE = 64
F32 = jnp.float32
BF16 = jnp.bfloat16
BLK = 32


def dft_blocks():
    counter = np.arange(SIDE)
    phase = (np.outer(counter, counter) % SIDE) * (2.0 * np.pi / SIDE)
    real = np.cos(phase) / np.sqrt(SIDE)
    imag = -np.sin(phase) / np.sqrt(SIDE)
    left = np.block([[real, -imag], [imag, real]])
    right = np.block([[real, imag], [-imag, real]])
    return left.astype(np.float32).astype(jnp.bfloat16), right.astype(np.float32).astype(jnp.bfloat16)


class Sems:
    def __init__(self, send, recv):
        self.send, self.recv, self.used, self.started, self.now = send, recv, 0, [], -5.0

    def make(self, src, dst, dev):
        i = self.used
        self.used += 1
        copy = pltpu.make_async_remote_copy(
            src_ref=src,
            dst_ref=dst,
            send_sem=self.send.at[i],
            recv_sem=self.recv.at[i],
            device_id=dev,
            device_id_type=pl.DeviceIdType.MESH,
        )
        return copy

    def start(self, src, dst, dev):
        copy = self.make(src, dst, dev)
        copy.start()
        self.started.append((copy, self.now))
        return copy

    def settle(self, now):
        old = [copy for copy, at in self.started if at + 5.5 < now]
        self.started = [(copy, at) for copy, at in self.started if at + 5.5 >= now]
        for copy in old:
            copy.wait_send()


N_SEMS = 288
Z_ORDER = (4, 3, 5, 2, 6, 1, 7, 0)


def rows(start, size):
    return pl.ds(pl.multiple_of(start, 8), size)


def shifted(blocks, rest):
    turned = pltpu.roll(blocks, (16 - rest) % 8, axis=1)
    row = lax.broadcasted_iota(jnp.int32, turned[1:].shape, 1)
    return jnp.where(row < 8 - rest, turned[:-1], turned[1:])


def kernel(
    row_ref, col_ref, cnt_ref, obj_hbm, probe_hbm, amp_hbm, lf_hbm, rf_hbm,
    onew_ref, pnew_ref,
    obj, probe_ref, amp_ref, lf_ref, rf_ref,
    border, win, psi, half, spec, power, pw, factor, pad, pgrad, p_core,
    px, pz, own, edge, from_core, ro, re, arrive,
    send_sem, recv_sem, fetch_sem, known,
):
    t = lax.axis_index("tile")
    y = lax.axis_index("mode")
    core = t % 2
    z = (t // 2) % NZ
    x = t // (2 * NZ)
    sems = Sems(send_sem, recv_sem)

    def tile_dev(xx, zz, cc):
        return ((xx * NZ + zz) * 2 + cc, y)

    t_left = ((t + N_TILE - 1) % N_TILE, y)
    t_right = ((t + 1) % N_TILE, y)
    peer = tile_dev(x, z, 1 - core)

    y_on = [(t, (y + k) % NY) for k in range(1, NY)]
    x_on = [tile_dev((x + k) % NX, z, core) for k in range(1, NX)]
    z_dev = [tile_dev(x, (z + k) % NZ, core) for k in range(1, NZ)]

    def tell(semaphore, devices):
        for dev in devices:
            pl.semaphore_signal(semaphore, inc=1, device_id=dev, device_id_type=pl.DeviceIdType.MESH)

    barrier = pltpu.get_barrier_semaphore()
    z_next = [z_dev[0], z_dev[-1]]
    near_by = [y_on[0], y_on[2], x_on[0], x_on[2], *z_next]
    tell(barrier, [t_left, t_right, *near_by])
    fetch = []
    for src, dst in ((obj_hbm, obj), (probe_hbm, probe_ref), (lf_hbm, lf_ref), (rf_hbm, rf_ref), (amp_hbm, amp_ref)):
        fetch.append(pltpu.make_async_copy(src, dst, fetch_sem.at[len(fetch)]))
        fetch[-1].start()
    pl.semaphore_wait(barrier, 2 + len(near_by))
    tell(known.at[0], near_by)

    def blocks(index, first, last):
        return pl.ds(index * (ROWS // 32) + first, last - first)

    def near(ref, at):
        return ref.at[:, at]

    y_up, y_across, y_down = [(y + k) % NY for k in range(1, NY)]
    whole = sems.make(obj_hbm, border, peer)
    relayed = [blocks(y, 3 * i, 3 * i + 3) for i in range(3)]
    ranges = (*relayed, blocks(y_across, 0, 12), *(blocks(i, 9, 12) for i in (y, y_up, y_down)))
    direct = [sems.make(near(obj_hbm, at), near(border, at), t_left) for at in ranges]
    passed = [sems.make(near(border, at), near(border, at), dev) for at in relayed for dev in (y_on[0], y_on[2])]

    @pl.when(core == 1)
    def _():
        whole.start()

    @pl.when(core == 0)
    def _():
        for copy in direct:
            copy.start()

    for s in range(SCANS):
        for c in range(2):
            pad[s, c, 0:16] = jnp.zeros((16, 8, SIDE), F32)
            pad[s, c, 48:64] = jnp.zeros((16, 8, SIDE), F32)

    for copy in fetch:
        copy.wait()

    @pl.when(core == 1)
    def _():
        for i in range(3):
            direct[i].wait_recv()
            passed[2 * i].start()
            passed[2 * i + 1].start()
        for copy in (*direct[3:], *passed):
            copy.wait_recv()

    @pl.when(core == 0)
    def _():
        whole.wait_recv()

    pl.semaphore_wait(known.at[0], len(near_by))
    tell(known.at[1], z_next)

    lane = lax.broadcasted_iota(jnp.int32, (BLK // 8 + 1, 8, SIDE), 2)
    beyond = jnp.where(t == N_TILE - 1, 0.0, 1.0).astype(F32)

    def forward(s):
        top, col = row_ref[s], col_ref[s]
        base = jnp.minimum(top // 8, 15)
        rest = top - base * 8

        def cut(i, carry):
            at = pl.ds(base + i * (BLK // 8), BLK // 8 + 1)
            for c in range(2):
                block = jnp.where(lane >= col, obj[c, at], border[c, at] * beyond)
                block = pltpu.roll(shifted(block, rest), (SIDE - col) % SIDE, axis=2)
                win[s, c, rows(i * BLK, BLK), :] = block.reshape(BLK, SIDE)
            return carry

        lax.fori_loop(0, SIDE // BLK, cut, 0, unroll=8)

        def mode(m):
            pr, pi = probe_ref[m, 0].reshape(SIDE, SIDE), probe_ref[m, 1].reshape(SIDE, SIDE)
            wr, wi = win[s, 0], win[s, 1]
            psi[m, 0:SIDE, :] = (pr * wr - pi * wi).astype(BF16)
            psi[m, SIDE:, :] = (pr * wi + pi * wr).astype(BF16)
            mid = jnp.dot(lf_ref[...], psi[m], preferred_element_type=F32).astype(BF16)
            half[m, :, 0:SIDE] = mid[0:SIDE]
            half[m, :, SIDE:] = mid[SIDE:]
            out = jnp.dot(half[m], rf_ref[...], preferred_element_type=F32).astype(BF16)
            spec[s, m] = out
            wide = out.astype(F32)
            wide = wide * wide
            wide = wide[:, :SIDE] + wide[:, SIDE:]
            power[s] = wide if m == 0 else power[s] + wide

        for m in range(MODES):
            mode(m)

    n_q = SIDE // NY

    def q_rows(index):
        return rows(index * n_q, n_q)

    sums = []
    for s in range(SCANS):
        forward(s)
        sums.append([])
        for k in (2, 1, 3):
            src = power.at[s, q_rows((y + k) % NY), :]
            sums[s].append(sems.start(src, pw.at[s, k - 1], y_on[k - 1]))
    gathers = []
    for s in range(SCANS):
        for copy in sums[s]:
            copy.wait_recv()
        active = jnp.where(s < cnt_ref[0], 1.0, 0.0).astype(F32)
        q = q_rows(y)
        total = power[s, q, :] + pw[s, 0] + pw[s, 1] + pw[s, 2]
        factor[s, q, :] = amp_ref[s, q, :] / jnp.maximum(jnp.sqrt(total), 0.5) - 1.0
        factor[s, q, :] = factor[s, q, :] * active
        gathers.append([sems.start(factor.at[s, q, :], factor.at[s, q, :], y_on[k - 1]) for k in (2, 1, 3)])
    pl.semaphore_wait(known.at[1], 2)
    tell(known.at[2], z_next)

    def backward(s):
        def mode(m):
            f = factor[s]
            psi[m, 0:SIDE, :] = (spec[s, m, :, :SIDE].astype(F32) * f).astype(BF16)
            psi[m, SIDE:, :] = (spec[s, m, :, SIDE:].astype(F32) * f).astype(BF16)
            mid = jnp.dot(rf_ref[...], psi[m], preferred_element_type=F32).astype(BF16)
            half[m, :, 0:SIDE] = mid[0:SIDE]
            half[m, :, SIDE:] = mid[SIDE:]
            chi = jnp.dot(half[m], lf_ref[...], preferred_element_type=F32)
            cr, ci = chi[:, :SIDE], chi[:, SIDE:]
            pr, pi = probe_ref[m, 0].reshape(SIDE, SIDE), probe_ref[m, 1].reshape(SIDE, SIDE)
            wr, wi = win[s, 0], win[s, 1]
            gr = (pr * cr + pi * ci).reshape(SIDE // 8, 8, SIDE)
            gi = (pr * ci - pi * cr).reshape(SIDE // 8, 8, SIDE)
            pad[s, 0, 16:48] = gr if m == 0 else pad[s, 0, 16:48] + gr
            pad[s, 1, 16:48] = gi if m == 0 else pad[s, 1, 16:48] + gi
            pgr = (wr * cr + wi * ci).reshape(NZ, NX, 8, SIDE)
            pgi = (wr * ci - wi * cr).reshape(NZ, NX, 8, SIDE)
            if s == 0:
                pgrad[m, 0] = pgr
                pgrad[m, 1] = pgi
            else:
                pgrad[m, 0] = pgrad[m, 0] + pgr
                pgrad[m, 1] = pgrad[m, 1] + pgi

        return mode

    def place(s):
        col, down = col_ref[s], 128 - row_ref[s]
        base = jnp.minimum(down // 8, 15)

        def rows_of(i, carry):
            at = rows(i * BLK, BLK)
            for c in range(2):
                block = pad[s, c, pl.ds(base + i * (BLK // 8), BLK // 8 + 1)]
                block = pltpu.roll(shifted(block, down - base * 8), col, axis=2)
                here = lane[1:] >= col
                inside = jnp.where(here, block, 0.0).reshape(BLK, SIDE)
                outside = jnp.where(here, 0.0, block).reshape(BLK, SIDE)
                own[c, at, :] = inside if s == 0 else own[c, at, :] + inside
                edge[c, at, :] = outside if s == 0 else edge[c, at, :] + outside
            return carry

        lax.fori_loop(0, ROWS // BLK, rows_of, 0, unroll=12)

    core_sum = []
    for s in range(SCANS):
        for copy in gathers[s]:
            copy.wait_recv()
        mode = backward(s)
        for m in range(MODES):
            mode(m)
            if s == SCANS - 1:
                core_sum.append(sems.start(pgrad.at[m, 1 - core], p_core.at[m], peer))
        if s < SCANS - 1:
            place(s)

    quarter_rows = ROWS // NY

    def quarter(index):
        return rows(index * quarter_rows, quarter_rows)

    def object_flow():
        yield 0.5
        place(SCANS - 1)

        core_edge = sems.make(edge, from_core, peer)
        far = (2, 1, 3)
        edge_sum = [sems.make(edge.at[:, quarter((y + k) % NY), :], re.at[k - 1], y_on[k - 1]) for k in far]
        n_cross = 4
        n_part = quarter_rows // n_cross
        cross = []
        for c in range(2):
            for i in range(n_cross):
                src = edge.at[c, rows(y * quarter_rows + i * n_part, n_part), :]
                cross.append(sems.make(src, arrive.at[c, rows(i * n_part, n_part), :], t_right))
        own_sum = {}
        for c in range(2):
            for k in far:
                src = own.at[c, quarter((y + k) % NY), :]
                own_sum[c, k] = sems.make(src, ro.at[k - 1, c], y_on[k - 1])
        spread = {}
        for c in range(2):
            here = onew_ref.at[c, quarter(y), :]
            for k in far:
                spread[c, k] = sems.make(here, here, y_on[k - 1])
        q8 = pl.ds(y * (quarter_rows // 8), quarter_rows // 8)
        inner = jnp.where(t == 0, 0.0, 1.0).astype(F32)

        def finish(c, on_core):
            @pl.when(core == on_core)
            def _():
                if on_core == 0:
                    for copy in cross[c * n_cross : (c + 1) * n_cross]:
                        copy.wait_recv()
                for k in far:
                    own_sum[c, k].wait_recv()
                total = own[c, quarter(y), :] + ro[0, c] + ro[1, c] + ro[2, c]
                if on_core == 0:
                    total = total + arrive[c] * inner
                onew_ref[c, quarter(y), :] = obj[c, q8].reshape(quarter_rows, SIDE) + total
                for k in far:
                    spread[c, k].start()

        @pl.when(core == 0)
        def _():
            core_edge.start()

        @pl.when(core == 1)
        def _():
            for copy in edge_sum:
                copy.start()

        yield 4.5

        @pl.when(core == 0)
        def _():
            for copy in (*direct, core_edge):
                copy.wait_send()

        @pl.when(core == 1)
        def _():
            for copy in (whole, *passed):
                copy.wait_send()
            core_edge.wait_recv()
            own[...] = own[...] + from_core[...]

        for copy in own_sum.values():
            copy.start()
        sems.started += [(copy, sems.now + 8.0) for copy in own_sum.values()]
        yield 10.0

        @pl.when(core == 1)
        def _():
            for copy in edge_sum:
                copy.wait_recv()
            edge[:, quarter(y), :] = edge[:, quarter(y), :] + re[0] + re[1] + re[2]
            cross[0].start()

        for i in range(1, 2 * n_cross):
            yield 10.0 + 0.35 * i
            if i == 7:
                finish(0, 1)

            @pl.when(core == 1)
            def _(copy=cross[i]):
                copy.start()

        yield 15.6
        finish(0, 0)
        yield 16.4
        finish(1, 1)
        yield 18.2
        finish(1, 0)
        sems.started += [(copy, sems.now) for copy in spread.values()]

        @pl.when(core == 1)
        def _():
            for copy in (*edge_sum, *cross):
                copy.wait_send()

        yield 27.0
        for copy in spread.values():
            copy.wait_recv()

    def probe_flow(m):
        begin = 0.2 + 2.8 * m
        grad, new = pgrad.at[m, core], pnew_ref.at[m, core]
        yield 0.2 + 0.8 * m
        core_sum[m].wait_recv()
        grad[...] = grad[...] + p_core[m]
        x_sum, z_sum = {}, {}
        for k in Z_ORDER:
            for d in (2, 1, 3):
                src = grad.at[(z + k) % NZ, (x + d) % NX]
                x_sum[k, d] = sems.start(src, px.at[m, k, d - 1], x_on[d - 1])
        for j, k in enumerate(Z_ORDER):
            yield begin + 3.7 + 0.35 * j
            for d in (2, 1, 3):
                x_sum[k, d].wait_recv()
            zz = (z + k) % NZ
            grad[zz, x] = grad[zz, x] + px[m, k, 0] + px[m, k, 1] + px[m, k, 2]
            if k:
                z_sum[k] = sems.start(grad.at[zz, x], pz.at[m, k - 1], z_dev[k - 1])
        yield begin + 9.0
        total = grad[z, x]
        for k in Z_ORDER[:-1]:
            z_sum[k].wait_recv()
            total = total + pz[m, k - 1]
        new[z, x] = probe_ref[m, core, z, x] + total * 0.5

        def share(at, dev):
            return sems.start(new.at[at], new.at[at], dev)

        core_all = []
        z_all = {k: share((z, x), z_dev[k - 1]) for k in Z_ORDER[:-1]}
        x_all = {}
        for j, k in enumerate(Z_ORDER[::-1]):
            if k:
                yield begin + 11.8 + 0.3 * j
                z_all[k].wait_recv()
            for d in (2, 1, 3):
                x_all[k, d] = share(((z + NZ - k) % NZ, x), x_on[d - 1])
        for j, k in enumerate(Z_ORDER[::-1]):
            yield begin + 15.8 + 0.3 * j
            for d in (1, 3, 2):
                x_all[k, d].wait_recv()
            core_all.append(share(((z + NZ - k) % NZ,), peer))
        yield begin + 19.5
        for copy in core_all:
            copy.wait_recv()

    pl.semaphore_wait(known.at[2], 2)
    flows = [object_flow(), *(probe_flow(m) for m in range(MODES))]
    sems.now = 0.0
    due = [next(flow) for flow in flows]
    while flows:
        i = due.index(min(due))
        sems.now = due[i]
        sems.settle(sems.now)
        at = next(flows[i], None)
        if at is None:
            del flows[i], due[i]
        else:
            due[i] = at
    sems.settle(1000.0)


def on_device(object_tile, probe, amplitudes, row_offsets, col_offsets, scan_count):
    left, right = dft_blocks()
    vmem = pl.BlockSpec(memory_space=pltpu.VMEM)
    smem = pl.BlockSpec(memory_space=pltpu.SMEM)
    stacked = (MODES, 2, NZ, NX, 8, SIDE)
    anywhere = pl.BlockSpec(memory_space=pl.ANY)
    scratch = [
        pltpu.VMEM((2, ROWS // 8, 8, SIDE), F32),
        pltpu.VMEM(stacked, F32),
        pltpu.VMEM((SCANS, SIDE, SIDE), F32),
        pltpu.VMEM((2 * SIDE, 2 * SIDE), BF16),
        pltpu.VMEM((2 * SIDE, 2 * SIDE), BF16),
        pltpu.VMEM((2, ROWS // 8, 8, SIDE), F32),
        pltpu.VMEM((SCANS, 2, SIDE, SIDE), F32),
        pltpu.VMEM((MODES, 2 * SIDE, SIDE), BF16),
        pltpu.VMEM((MODES, SIDE, 2 * SIDE), BF16),
        pltpu.VMEM((SCANS, MODES, SIDE, 2 * SIDE), BF16),
        pltpu.VMEM((SCANS, SIDE, SIDE), F32),
        pltpu.VMEM((SCANS, NY - 1, SIDE // NY, SIDE), F32),
        pltpu.VMEM((SCANS, SIDE, SIDE), F32),
        pltpu.VMEM((SCANS, 2, 2 * SIDE // 8, 8, SIDE), F32),
        pltpu.VMEM(stacked, F32),
        pltpu.VMEM((MODES, NZ, NX, 8, SIDE), F32),
        pltpu.VMEM((MODES, NZ, NX - 1, 8, SIDE), F32),
        pltpu.VMEM((MODES, NZ - 1, 8, SIDE), F32),
        pltpu.VMEM((2, ROWS, SIDE), F32),
        pltpu.VMEM((2, ROWS, SIDE), F32),
        pltpu.VMEM((2, ROWS, SIDE), F32),
        pltpu.VMEM((NY - 1, 2, ROWS // NY, SIDE), F32),
        pltpu.VMEM((NY - 1, 2, ROWS // NY, SIDE), F32),
        pltpu.VMEM((2, ROWS // 4, SIDE), F32),
        pltpu.SemaphoreType.DMA((N_SEMS,)),
        pltpu.SemaphoreType.DMA((N_SEMS,)),
        pltpu.SemaphoreType.DMA((5,)),
        pltpu.SemaphoreType.REGULAR((3,)),
    ]
    object_new, probe_new = pl.pallas_call(
        kernel,
        out_shape=(
            pltpu.VMEM(object_tile.shape, F32),
            pltpu.VMEM(stacked, F32),
        ),
        in_specs=[smem] * 3 + [anywhere] * 5,
        out_specs=(vmem, vmem),
        scratch_shapes=scratch,
        compiler_params=pltpu.CompilerParams(
            collective_id=0, has_side_effects=True, vmem_limit_bytes=56 * 1024 * 1024
        ),
        cost_estimate=pl.CostEstimate(flops=3_300_000_000, bytes_accessed=6_000_000, transcendentals=131072),
    )(
        row_offsets,
        col_offsets,
        scan_count,
        object_tile.reshape(2, ROWS // 8, 8, SIDE),
        probe.reshape(stacked),
        amplitudes,
        jnp.asarray(left),
        jnp.asarray(right),
    )

    def leave(a, b, a_out, b_out, sem):
        copies = [pltpu.make_async_copy(src, dst, sem.at[i]) for i, (src, dst) in enumerate(((a, a_out), (b, b_out)))]
        for copy in copies:
            copy.start()
        for copy in copies:
            copy.wait()

    object_new, probe_new = pl.pallas_call(
        leave,
        out_shape=(jax.ShapeDtypeStruct(object_tile.shape, F32), jax.ShapeDtypeStruct(stacked, F32)),
        in_specs=[anywhere] * 2,
        out_specs=(anywhere, anywhere),
        scratch_shapes=[pltpu.SemaphoreType.DMA((2,))],
        compiler_params=pltpu.CompilerParams(vmem_limit_bytes=16 * 1024 * 1024),
    )(object_new, probe_new)
    return object_new, probe_new.reshape(probe.shape)


def solution(mesh):
    in_specs = (
        P(None, None, "tile"),
        P("mode", None, None, None),
        P("tile", None, None),
        P("tile"),
        P("tile"),
        P("tile"),
    )
    out_specs = (P(None, None, "tile"), P("mode", None, None, None))
    return jax.shard_map(on_device, mesh=mesh, in_specs=in_specs, out_specs=out_specs, check_vma=False)
```
